32 devices in a mesh: frame: 16 (over z, y, core), pix: 2 (over x).
Axes of the slice: x: 2, y: 2, z: 4, core: 2. Of those that a mesh axis runs over, the one named last changes fastest.
Arguments:
- library: float32 [6144, 3072], P('frame', 'pix'), may hold values from -5000 to 5000
- annulus: int32 [1536], P('pix'), may hold values from 0 to 1535, as said below
Outputs:
- gram: float32 [6144, 6144], P('frame', 'pix')
The draws below stay inside these ranges and needn't reach their ends.
Inputs may be any that keep to these rules, and one draw needn't show every extreme that they name: `annulus`: within each aligned block of 768 entries the values are distinct and rising, and each block holds both 0 and 1535.
All inputs are finite; a program needn't handle non-finite values.
Results may differ from the reference program's by a relative error of at most 0.000065.
Values sent between devices are 32-bit elements; how exact they have to be, the bound alone decides.
No kernel may reach another device: no remote copies, remote signals or barrier semaphores. Data moves between devices by JAX's collectives and lax.ppermute only.
A program may use at most 128 MiB of HBM per device.

```python
import math
import jax
import jax.numpy as jnp
from jax import lax

PIX = 1536
PIX_DEV = 768
BAND_DEV = 1536
BAND = 3072
FRAMES = 6144
N_PIX = 2


def draw_library(key, part):
    key = jax.random.fold_in(key, 11)
    keys = jax.random.split(key, 6)
    frame_scale = jnp.exp(jax.random.uniform(keys[0], (FRAMES,), jnp.float32) * math.log(10.0))
    column_rise = jnp.power(3.0, jnp.arange(BAND, dtype=jnp.float32) / (BAND - 1))
    column_amp = column_rise * jnp.exp(jax.random.uniform(keys[1], (BAND,), jnp.float32) * math.log(10.0))
    speckle = jnp.clip(jax.random.normal(keys[2], (BAND,), jnp.float32), -4.0, 4.0)
    offset = jnp.clip(jax.random.normal(keys[3], (FRAMES,), jnp.float32), -4.0, 4.0)
    common = jnp.clip(jax.random.normal(keys[4], (FRAMES,), jnp.float32), -4.0, 4.0)
    noise = jnp.clip(jax.random.normal(keys[5], (FRAMES, BAND), jnp.float32), -5.0, 5.0)
    inner = common[:, None] * speckle[None, :] + noise
    return frame_scale[:, None] * (offset[:, None] + column_amp[None, :] * inner)


def draw_annulus(key, part):
    key = jax.random.fold_in(key, 23)
    blocks = PIX // PIX_DEV
    block_keys = jax.random.split(key, blocks)

    def one_block(block_key):
        order = jax.random.permutation(block_key, BAND_DEV - 2).astype(jnp.int32) + 1
        chosen = order[:PIX_DEV - 2]
        ends = jnp.array([0, BAND_DEV - 1], dtype=jnp.int32)
        return jnp.sort(jnp.concatenate([ends, chosen]))
    return jax.vmap(one_block)(block_keys).reshape(PIX).astype(jnp.int32)


def setup_inputs(seed: int = 0) -> dict:
    splits = jax.random.split(jax.random.key(seed), 3)
    return {
        "library": draw_library(jax.random.fold_in(splits[2], 71), 0),
        "annulus": draw_annulus(jax.random.fold_in(splits[2], 71), 0),
    }


def reference(library, annulus):
    banded = library.reshape(FRAMES, N_PIX, BAND_DEV)
    where = jnp.broadcast_to(annulus.reshape(1, N_PIX, PIX_DEV), (FRAMES, N_PIX, PIX_DEV))
    picked = jnp.take_along_axis(banded, where, axis=2).reshape(FRAMES, PIX)
    frame_mean = lax.optimization_barrier(jnp.sum(picked, axis=1)) / PIX
    centered = picked - frame_mean[:, None]
    squares = lax.optimization_barrier(jnp.sum(centered * centered, axis=1))
    unit = centered / jnp.sqrt(squares + 1e-06)[:, None]
    return jnp.dot(unit, unit.T, precision=lax.Precision.HIGHEST, preferred_element_type=jnp.float32)
```

```python
import functools

import jax
import jax.numpy as jnp
from jax import lax
from jax.experimental import pallas as pl
from jax.experimental.pallas import tpu as pltpu
from jax.sharding import PartitionSpec as P

PIX = 1536
EPS = 1e-06
GROUPS = ((64, 64), (128,), (128,))
PIECES = tuple(rows for group in GROUPS for rows in group)
STAT_ROWS = 8
VMEM = 60 << 20
F32, BF16 = jnp.float32, jnp.bfloat16
NT = (((1,), (1,)), ((), ()))


def split(a):
    high = a.astype(BF16)
    return high, (a - high.astype(F32)).astype(BF16)


def dot_nt(high, low, b):
    b_high, b_low = split(b)
    dot = functools.partial(
        lax.dot_general, dimension_numbers=NT, preferred_element_type=F32
    )
    return dot(high, b_high) + (dot(high, b_low) + dot(low, b_high))


def pick_kernel(annulus_ref, library_ref, high_ref, low_ref, *piece_refs):
    rows, band = library_ref.shape
    pix = annulus_ref.shape[1]
    tile = 256
    width = band - pix + tile
    columns = []
    for start in range(0, pix, tile):
        a = library_ref[:, start : start + width]
        high, rest = split(a)
        mid, low = split(a - high.astype(F32))
        where = annulus_ref[:, start : start + tile] - start
        one_hot = jnp.where(
            lax.broadcasted_iota(jnp.int32, (width, tile), 0) == where, 1.0, 0.0
        ).astype(BF16)
        parts = jnp.dot(
            jnp.concatenate([high, mid, low], axis=0),
            one_hot,
            preferred_element_type=F32,
        )
        columns.append(
            parts[:rows] + parts[rows : 2 * rows] + parts[2 * rows :]
        )
    picked = jnp.concatenate(columns, axis=1)
    mean = jnp.sum(picked, axis=1, keepdims=True) / pix
    centered = picked - mean
    shift = jnp.sum(centered, axis=1, keepdims=True) / pix
    centered = centered - shift
    mean = mean + shift
    squares = jnp.sum(centered * centered, axis=1, keepdims=True)
    unit = centered / jnp.sqrt(squares + EPS)
    high_ref[...], low_ref[...] = split(unit)
    start = 0
    for ref, count in zip(piece_refs, PIECES):
        ref[:count] = unit[start : start + count]
        start += count
    first = piece_refs[0]
    count = PIECES[0]
    as_row = [
        jnp.transpose(jnp.broadcast_to(v, (rows, 128)))[:STAT_ROWS]
        for v in (mean, squares)
    ]
    first[count:] = jnp.concatenate(as_row, axis=1)


def pick(library, annulus):
    rows = library.shape[0]
    pix = annulus.shape[0]
    shapes = [jax.ShapeDtypeStruct((rows, pix), BF16)] * 2
    for i, count in enumerate(PIECES):
        shapes.append(
            jax.ShapeDtypeStruct((count + (STAT_ROWS if i == 0 else 0), pix), F32)
        )
    return pl.pallas_call(
        pick_kernel,
        out_shape=shapes,
        compiler_params=pltpu.CompilerParams(vmem_limit_bytes=VMEM),
        name="pick",
    )(annulus.reshape(1, pix), library)


def send_kernel(count, x_ref, high_ref, low_ref, gathered_ref, *refs):
    out_ref = refs[-1]
    b = gathered_ref[:, :count, :]
    b = b.reshape(-1, b.shape[-1])
    out_ref[0] = dot_nt(high_ref[...], low_ref[...], b)


def send_product(x, high, low, gathered, count, after):
    rows, pix = high.shape
    frames = gathered.shape[0]
    per = 256 // count
    steps = frames // 2 // per
    whole = lambda i, x: (0, 0)
    return pl.pallas_call(
        functools.partial(send_kernel, count),
        grid_spec=pltpu.PrefetchScalarGridSpec(
            num_scalar_prefetch=1,
            grid=(steps,),
            in_specs=[
                pl.BlockSpec((rows, pix), whole),
                pl.BlockSpec((rows, pix), whole),
                pl.BlockSpec(
                    (per, gathered.shape[1], pix),
                    lambda i, x: ((1 - x[0]) * steps + i, 0, 0),
                ),
            ]
            + [pl.BlockSpec(memory_space=pl.ANY)] * len(after),
            out_specs=pl.BlockSpec((1, rows, 256), lambda i, x: (i, 0, 0)),
        ),
        out_shape=jax.ShapeDtypeStruct((steps, rows, 256), F32),
        compiler_params=pltpu.CompilerParams(vmem_limit_bytes=VMEM),
        cost_estimate=pl.CostEstimate(
            flops=6 * rows * steps * 256 * pix,
            bytes_accessed=4 * steps * 256 * (pix + rows),
            transcendentals=0,
        ),
        name="send_product",
    )(x, high, low, gathered, *after)


def keep_kernel(group, index, x_ref, high_ref, low_ref, own_ref, stat_ref, *refs):
    n = len(group)
    gathered, received, out_ref = refs[:n], refs[n : 2 * n], refs[-1]
    b = [ref[0, :count, :] for ref, count in zip(gathered, group)]
    b = b[0] if n == 1 else jnp.concatenate(b, axis=0)
    kept = dot_nt(high_ref[...], low_ref[...], b)
    if n == 1:
        other = received[0][0]
    else:
        odd = lax.rem(pl.program_id(0), 2) == 1
        half = group[0]
        left = jnp.concatenate([ref[0][:, :half] for ref in received], axis=1)
        right = jnp.concatenate([ref[0][:, half:] for ref in received], axis=1)
        other = jnp.where(odd, right, left)
    at = slice(128 * index, 128 * index + 128)
    own, stat = own_ref[...], stat_ref[0]
    out_ref[...] = (
        own[:, 0:1] * stat[0:1, at] * kept
        + own[:, 1:2] * stat[1:2, at] * other
        + own[:, 2:3] * stat[2:3, at]
    )


def keep_product(x, high, low, own, stats, gathered, received, group, index, out):
    rows, pix = high.shape
    frames = gathered[0].shape[0] // 2
    whole = lambda i, x: (0, 0)
    in_specs = [
        pl.BlockSpec((rows, pix), whole),
        pl.BlockSpec((rows, pix), whole),
        pl.BlockSpec(own.shape, whole),
        pl.BlockSpec((1,) + stats.shape[1:], lambda i, x: (x[0] * frames + i, 0, 0)),
    ]
    for g in gathered:
        in_specs.append(
            pl.BlockSpec((1,) + g.shape[1:], lambda i, x: (x[0] * frames + i, 0, 0))
        )
    for count in group:
        if count == 128:
            at = lambda i, x: (i // 2, 0, lax.rem(i, 2))
        else:
            at = lambda i, x: (i // 4, 0, lax.rem(i // 2, 2))
        in_specs.append(pl.BlockSpec((1, rows, 128), at))
    operands = [x, high, low, own, stats, *gathered, *received]
    alias = {}
    if out is not None:
        in_specs.append(pl.BlockSpec(memory_space=pl.ANY))
        alias = {len(operands): 0}
        operands.append(out)
    return pl.pallas_call(
        functools.partial(keep_kernel, group, index),
        grid_spec=pltpu.PrefetchScalarGridSpec(
            num_scalar_prefetch=1,
            grid=(frames,),
            in_specs=in_specs,
            out_specs=pl.BlockSpec(
                (rows, 128), lambda i, x: (0, i * (rows // 128) + index)
            ),
        ),
        out_shape=jax.ShapeDtypeStruct((rows, frames * rows), F32),
        input_output_aliases=alias,
        compiler_params=pltpu.CompilerParams(vmem_limit_bytes=VMEM),
        cost_estimate=pl.CostEstimate(
            flops=6 * rows * frames * 128 * pix,
            bytes_accessed=4 * frames * 128 * (pix + 2 * rows),
            transcendentals=0,
        ),
        name="keep_product",
    )(*operands)


def scales(mine, other, frame, rows, pix):
    both = jnp.stack([mine, other])
    mean, squares = both[:, :, :rows], both[:, :, rows:]
    gap = (mean[0] - mean[1]) / 2
    total = squares[0] + squares[1] + (2 * pix) * (gap * gap)
    length = jnp.sqrt(total + EPS)
    part = jnp.sqrt(squares + EPS) / length
    stats = jnp.stack([part[0], part[1], (2 * pix) ** 0.5 * gap / length], axis=1)
    own = lax.dynamic_index_in_dim(stats, frame, 0, keepdims=False).T
    return jnp.pad(own, ((0, 0), (0, 125))), jnp.pad(stats, ((0, 0), (0, 5), (0, 0)))


def local_pair(library, annulus):
    rows = library.shape[0]
    pix = annulus.shape[0]
    swap = [(0, 1), (1, 0)]
    x = lax.axis_index("pix").astype(jnp.int32).reshape(1)
    high, low, *pieces = pick(library, annulus)
    gathered = [lax.all_gather(p, "frame", axis=0) for p in pieces]
    mine = gathered[0][:, PIECES[0], :]
    received, after = [], []
    for g, count in zip(gathered, PIECES):
        product = send_product(x, high, low, g, count, after)
        after = [product] + received[-1:]
        received.append(lax.ppermute(product, "pix", swap))
    other = lax.ppermute(mine, "pix", swap)
    own, stats = scales(mine, other, lax.axis_index("frame"), rows, pix)
    out, at = None, 0
    for index, group in enumerate(GROUPS):
        n = len(group)
        out = keep_product(
            x, high, low, own, stats,
            gathered[at : at + n], received[at : at + n], group, index, out,
        )
        at += n
    return out


def local(library, annulus):
    picked = jnp.take(library, annulus, axis=1)
    total = lax.psum(jnp.sum(picked, axis=1), "pix")
    frame_mean = total / PIX
    centered = picked - frame_mean[:, None]
    squares = lax.psum(jnp.sum(centered * centered, axis=1), "pix")
    unit = centered / jnp.sqrt(squares + EPS)[:, None]
    partial_gram = lax.dot_general(
        unit,
        lax.all_gather(unit, "frame", axis=0, tiled=True),
        (((1,), (1,)), ((), ())),
        precision=lax.Precision.HIGHEST,
        preferred_element_type=jnp.float32,
    )
    return lax.psum_scatter(partial_gram, "pix", scatter_dimension=1, tiled=True)


def solution(mesh):
    placed = (P("frame", "pix"), P("pix"))
    pair = mesh.shape["pix"] == 2 and mesh.shape["frame"] % 8 == 0
    return jax.shard_map(
        local_pair if pair else local,
        mesh=mesh, in_specs=placed, out_specs=P("frame", "pix"), check_vma=False,
    )
```

```python
import functools

import jax
import jax.numpy as jnp
from jax import lax
from jax.experimental import pallas as pl
from jax.experimental.pallas import tpu as pltpu
from jax.sharding import PartitionSpec as P

PIX = 1536
EPS = 1e-06
STEP = 128
STAT_ROWS = 8
VMEM = 56 << 20
F32, BF16 = jnp.float32, jnp.bfloat16


def split(a):
    high = a.astype(BF16)
    return high, (a - high.astype(F32)).astype(BF16)


def pick_kernel(annulus_ref, library_ref, centered_ref, stat_ref):
    rows, band = library_ref.shape
    pix = annulus_ref.shape[1]
    tile = 256
    width = band - pix + tile
    columns = []
    for start in range(0, pix, tile):
        a = library_ref[:, start : start + width]
        high, rest = split(a)
        mid, low = split(a - high.astype(F32))
        where = annulus_ref[:, start : start + tile] - start
        one_hot = jnp.where(
            lax.broadcasted_iota(jnp.int32, (width, tile), 0) == where, 1.0, 0.0
        ).astype(BF16)
        parts = jnp.dot(
            jnp.concatenate([high, mid, low], axis=0),
            one_hot,
            preferred_element_type=F32,
        )
        columns.append(
            parts[:rows] + parts[rows : 2 * rows] + parts[2 * rows :]
        )
    picked = jnp.concatenate(columns, axis=1)
    mean = jnp.sum(picked, axis=1, keepdims=True) / pix
    centered = picked - mean
    shift = jnp.sum(centered, axis=1, keepdims=True) / pix
    centered = centered - shift
    mean = mean + shift
    squares = jnp.sum(centered * centered, axis=1, keepdims=True)
    centered_ref[...] = centered
    as_row = [
        jnp.transpose(jnp.broadcast_to(v, (rows, 128)))[:STAT_ROWS]
        for v in (mean, squares)
    ]
    stat_ref[...] = jnp.concatenate(as_row, axis=1)


def pick(library, annulus):
    rows = library.shape[0]
    pix = annulus.shape[0]
    return pl.pallas_call(
        pick_kernel,
        out_shape=[
            jax.ShapeDtypeStruct((rows, pix), F32),
            jax.ShapeDtypeStruct((STAT_ROWS, 2 * rows), F32),
        ],
        compiler_params=pltpu.CompilerParams(vmem_limit_bytes=VMEM),
        name="pick",
    )(annulus.reshape(1, pix), library)


def unit_kernel(centered_ref, mine_ref, other_ref, unit_ref, *piece_refs):
    rows, pix = centered_ref.shape
    mine, other = mine_ref[0:1], other_ref[0:1]
    gap = (mine[:, :rows] - other[:, :rows]) / 2
    squares = mine[:, rows:] + other[:, rows:] + (2 * pix) * (gap * gap)
    length = jnp.sqrt(squares + EPS)
    gap, length = [
        jnp.transpose(jnp.broadcast_to(v, (128, rows)))[:, :1] for v in (gap, length)
    ]
    unit = (centered_ref[...] + gap) / length
    unit_ref[...] = unit
    for k, ref in enumerate(piece_refs):
        ref[...] = unit[k * STEP : (k + 1) * STEP]


def units(centered, mine, other):
    rows, pix = centered.shape
    return pl.pallas_call(
        unit_kernel,
        out_shape=[jax.ShapeDtypeStruct((rows, pix), F32)]
        + [jax.ShapeDtypeStruct((STEP, pix), F32)] * (rows // STEP),
        compiler_params=pltpu.CompilerParams(vmem_limit_bytes=VMEM),
        name="unit",
    )(centered, mine, other)


def rows_kernel(a_ref, b_ref, high_ref, low_ref):
    pix = a_ref.shape[1]
    high_ref[:, :pix], low_ref[:, :pix] = split(a_ref[...])
    high_ref[:, pix:], low_ref[:, pix:] = split(b_ref[...])


def split_rows(a, b):
    rows, pix = a.shape
    return pl.pallas_call(
        rows_kernel,
        out_shape=[jax.ShapeDtypeStruct((rows, 2 * pix), BF16)] * 2,
        compiler_params=pltpu.CompilerParams(vmem_limit_bytes=VMEM),
        cost_estimate=pl.CostEstimate(
            flops=6 * rows * pix, bytes_accessed=16 * rows * pix, transcendentals=0
        ),
        name="split_rows",
    )(a, b)


def product_kernel(n, choice_ref, *refs):
    row_refs, refs = refs[: 2 * n], refs[2 * n :]
    column_refs, out_ref = refs[:6], refs[6]
    here, there = [], []
    for j in range(2):
        near, far, received = column_refs[3 * j : 3 * j + 3]
        here.append(jnp.where(choice_ref[j] == 1, near[...], far[...]))
        there.append(received[...])
    columns = jnp.concatenate(
        [jnp.concatenate(here, axis=0), jnp.concatenate(there, axis=0)], axis=1
    )
    high, low = split(jnp.transpose(columns))
    for i in range(n):
        a_high, a_low = row_refs[2 * i][...], row_refs[2 * i + 1][...]
        rows = a_high.shape[0]
        both = jnp.dot(
            jnp.concatenate([a_high, a_low], axis=0), high, preferred_element_type=F32
        )
        cross = jnp.dot(a_high, low, preferred_element_type=F32)
        out_ref[i] = both[:rows] + (both[rows:] + cross)


def product(choice, rows, columns):
    n = len(rows) // 2
    count, depth = rows[0].shape
    vmem = pl.BlockSpec(memory_space=pltpu.VMEM)
    return pl.pallas_call(
        functools.partial(product_kernel, n),
        in_specs=[pl.BlockSpec(memory_space=pltpu.SMEM)]
        + [vmem] * (len(rows) + len(columns)),
        out_specs=vmem,
        out_shape=jax.ShapeDtypeStruct((n, count, 2 * STEP), F32),
        compiler_params=pltpu.CompilerParams(vmem_limit_bytes=VMEM),
        cost_estimate=pl.CostEstimate(
            flops=6 * n * count * 2 * STEP * depth,
            bytes_accessed=4 * n * count * depth + 4 * n * count * 2 * STEP,
            transcendentals=0,
        ),
        name="product",
    )(choice, *rows, *columns)


def place_kernel(at_ref, own_ref, y_ref, core_ref, both_ref, *refs):
    out_ref = refs[-1]
    source = lax.rem(pl.program_id(0), 4)
    for s, ref in enumerate((own_ref, core_ref, y_ref, both_ref)):

        @pl.when(source == s)
        def _():
            out_ref[...] = ref[0]


def place(at, own, from_y, from_core, from_both, frames, out):
    rows = own.shape[1]
    block = pl.BlockSpec((1, rows, STEP), lambda i, at: (0, 0, i // 4))
    operands = [at, own, from_y, from_core, from_both]
    in_specs = [block] * 4
    alias = {}
    if out is not None:
        in_specs.append(pl.BlockSpec(memory_space=pl.ANY))
        alias = {len(operands): 0}
        operands.append(out)
    return pl.pallas_call(
        place_kernel,
        grid_spec=pltpu.PrefetchScalarGridSpec(
            num_scalar_prefetch=1,
            grid=(8,),
            in_specs=in_specs,
            out_specs=pl.BlockSpec((rows, STEP), lambda i, at: (0, at[i])),
        ),
        out_shape=jax.ShapeDtypeStruct((rows, frames * rows), F32),
        input_output_aliases=alias,
        compiler_params=pltpu.CompilerParams(vmem_limit_bytes=VMEM),
        cost_estimate=pl.CostEstimate(
            flops=0, bytes_accessed=8 * rows * STEP * 8, transcendentals=0
        ),
        name="place",
    )(*operands)


def local_pair(library, annulus):
    rows = library.shape[0]
    frames = lax.axis_size("frame")
    frame = lax.axis_index("frame")
    x = lax.axis_index("pix")
    z = frame // 4

    def swap_x(a):
        return lax.ppermute(a, "pix", [(0, 1), (1, 0)])

    def swap_y(a):
        return lax.ppermute(a, "frame", [(f, f ^ 2) for f in range(frames)])

    def swap_core(a):
        return lax.ppermute(a, "frame", [(f, f ^ 1) for f in range(frames)])

    def next_z(a):
        return lax.ppermute(a, "frame", [(f, (f + 4) % frames) for f in range(frames)])

    centered, stat = pick(library, annulus)
    unit, *pieces = units(centered, stat, swap_x(stat))

    ring = [[p] for p in pieces]
    for _ in range(3):
        for blocks in ring:
            blocks.append(next_z(blocks[-1]))

    unit_x = swap_x(unit)
    mine = [unit, unit_x]
    far = [swap_y(a) for a in mine]
    near_rows = split_rows(*mine) + split_rows(*[swap_core(a) for a in mine])
    far_rows = split_rows(*far) + split_rows(*[swap_core(a) for a in far])

    choice = jnp.stack([((z - j) % 4) // 2 == x for j in range(2)]).astype(jnp.int32)
    places = jnp.stack(
        [
            (((z - j) % 2) * 4 + ((frame % 4) ^ s)) * (rows // STEP)
            for j in range(2)
            for s in range(4)
        ]
    ).astype(jnp.int32)
    out = None
    for k, blocks in enumerate(ring):
        columns = []
        for j in range(2):
            send = jnp.where(choice[j] == 1, blocks[j + 2], blocks[j])
            columns += [blocks[j], blocks[j + 2], swap_x(send)]
        near = product(choice, near_rows, columns)
        far = swap_y(product(choice, far_rows, columns))
        from_core = swap_core(near[1:])
        from_both = swap_core(far[1:])
        out = place(places + k, near, far, from_core, from_both, frames // 2, out)
    return out


def local(library, annulus):
    picked = jnp.take(library, annulus, axis=1)
    total = lax.psum(jnp.sum(picked, axis=1), "pix")
    frame_mean = total / PIX
    centered = picked - frame_mean[:, None]
    squares = lax.psum(jnp.sum(centered * centered, axis=1), "pix")
    unit = centered / jnp.sqrt(squares + EPS)[:, None]
    partial_gram = lax.dot_general(
        unit,
        lax.all_gather(unit, "frame", axis=0, tiled=True),
        (((1,), (1,)), ((), ())),
        precision=lax.Precision.HIGHEST,
        preferred_element_type=jnp.float32,
    )
    return lax.psum_scatter(partial_gram, "pix", scatter_dimension=1, tiled=True)


def solution(mesh):
    placed = (P("frame", "pix"), P("pix"))
    pair = mesh.shape["pix"] == 2 and mesh.shape["frame"] == 16
    return jax.shard_map(
        local_pair if pair else local,
        mesh=mesh, in_specs=placed, out_specs=P("frame", "pix"), check_vma=False,
    )
```

```python
import functools

import jax
import jax.numpy as jnp
from jax import lax
from jax.experimental import pallas as pl
from jax.experimental.pallas import tpu as pltpu
from jax.sharding import PartitionSpec as P

PIX = 1536
EPS = 1e-06
STEP = 128
STAT_ROWS = 8
VMEM = 28 << 20
F32, BF16 = jnp.float32, jnp.bfloat16


def split(a):
    high = a.astype(BF16)
    return high, (a - high.astype(F32)).astype(BF16)


def pick_kernel(annulus_ref, library_ref, *piece_refs):
    rows, band = library_ref.shape
    pix = annulus_ref.shape[1]
    tile = 256
    width = band - pix + tile
    columns = []
    for start in range(0, pix, tile):
        a = library_ref[:, start : start + width]
        high, rest = split(a)
        mid, low = split(a - high.astype(F32))
        where = annulus_ref[:, start : start + tile] - start
        one_hot = jnp.where(
            lax.broadcasted_iota(jnp.int32, (width, tile), 0) == where, 1.0, 0.0
        ).astype(BF16)
        parts = jnp.dot(
            jnp.concatenate([high, mid, low], axis=0),
            one_hot,
            preferred_element_type=F32,
        )
        columns.append(
            parts[:rows] + parts[rows : 2 * rows] + parts[2 * rows :]
        )
    picked = jnp.concatenate(columns, axis=1)
    mean = jnp.sum(picked, axis=1, keepdims=True) / pix
    centered = picked - mean
    shift = jnp.sum(centered, axis=1, keepdims=True) / pix
    centered = centered - shift
    mean = mean + shift
    squares = jnp.sum(centered * centered, axis=1, keepdims=True)
    as_row = [
        jnp.transpose(jnp.broadcast_to(v, (rows, 128)))[:STAT_ROWS]
        for v in (mean, squares)
    ]
    for k, ref in enumerate(piece_refs):
        ref[:STEP] = centered[k * STEP : (k + 1) * STEP]
    piece_refs[0][STEP:] = jnp.concatenate(as_row, axis=1)


def pick(library, annulus):
    rows = library.shape[0]
    pix = annulus.shape[0]
    return pl.pallas_call(
        pick_kernel,
        out_shape=[
            jax.ShapeDtypeStruct((STEP + (STAT_ROWS if k == 0 else 0), pix), F32)
            for k in range(rows // STEP)
        ],
        compiler_params=pltpu.CompilerParams(vmem_limit_bytes=VMEM),
        name="pick",
    )(annulus.reshape(1, pix), library)


def normalize(a, b, a_stat, b_stat, k):
    pix = a.shape[1]
    rows = a_stat.shape[1] // 2
    mean = slice(k * STEP, (k + 1) * STEP)
    squares = slice(rows + k * STEP, rows + (k + 1) * STEP)
    gap = (a_stat[:, mean] - b_stat[:, mean]) / 2
    total = a_stat[:, squares] + b_stat[:, squares] + (2 * pix) * (gap * gap)
    scale = 1 / jnp.sqrt(total + EPS)
    gap, scale = [
        jnp.transpose(jnp.broadcast_to(v, (STEP, STEP)))[:, :1] for v in (gap, scale)
    ]
    return jnp.concatenate([(a + gap) * scale, (b - gap) * scale], axis=1)


def rows_kernel(*refs):
    out_ref = refs[-1]
    n = len(refs) // 2
    a_refs, b_refs = refs[:n], refs[n : 2 * n]
    a_stat, b_stat = a_refs[0][STEP : STEP + 1], b_refs[0][STEP : STEP + 1]
    for k in range(n):
        unit = normalize(a_refs[k][:STEP], b_refs[k][:STEP], a_stat, b_stat, k)
        high, low = split(unit)
        out_ref[k * STEP : (k + 1) * STEP] = high
        out_ref[(n + k) * STEP : (n + k + 1) * STEP] = low


def unit_rows(a, b):
    rows, pix = len(a) * STEP, a[0].shape[1]
    return pl.pallas_call(
        rows_kernel,
        out_shape=jax.ShapeDtypeStruct((2 * rows, 2 * pix), BF16),
        compiler_params=pltpu.CompilerParams(vmem_limit_bytes=VMEM),
        cost_estimate=pl.CostEstimate(
            flops=6 * rows * pix, bytes_accessed=16 * rows * pix, transcendentals=0
        ),
        name="unit_rows",
    )(*a, *b)


def product_kernel(k, *refs):
    rows_refs, refs = refs[:2], refs[2:]
    columns, stats, outs = refs[:4], refs[4:-2], refs[-2:]
    if k == 0:
        stats = [ref[STEP : STEP + 1] for ref in columns]
    else:
        stats = [ref[0:1] for ref in stats]
    unit = jnp.concatenate(
        [
            normalize(columns[c][:STEP], columns[c + 1][:STEP], stats[c], stats[c + 1], k)
            for c in (0, 2)
        ],
        axis=0,
    )
    high, low = split(unit)
    dot = functools.partial(
        lax.dot_general,
        dimension_numbers=(((1,), (1,)), ((), ())),
        preferred_element_type=F32,
    )
    for rows_ref, out_ref in zip(rows_refs, outs):
        rows = rows_ref.shape[0] // 2
        both = dot(rows_ref[...], high)
        out_ref[...] = both[:rows] + (both[rows:] + dot(rows_ref[:rows], low))


def product(k, near, far, columns, first):
    count, depth = near.shape
    vmem = pl.BlockSpec(memory_space=pltpu.VMEM)
    in_specs = [vmem] * 6
    operands = [near, far, *columns]
    if k:
        pix = depth // 2
        in_specs += [
            pl.BlockSpec((STAT_ROWS, pix), lambda i: (STEP // STAT_ROWS, 0))
        ] * 4
        operands += first
    out = jax.ShapeDtypeStruct((count // 2, 2 * STEP), F32)
    return pl.pallas_call(
        functools.partial(product_kernel, k),
        grid=(1,),
        in_specs=in_specs,
        out_specs=[vmem] * 2,
        out_shape=[out] * 2,
        compiler_params=pltpu.CompilerParams(vmem_limit_bytes=VMEM),
        cost_estimate=pl.CostEstimate(
            flops=6 * count * 2 * STEP * depth,
            bytes_accessed=4 * count * depth + 4 * count * 2 * STEP,
            transcendentals=0,
        ),
        name="product",
    )(*operands)


def place_kernel(at_ref, own_ref, far_ref, *refs):
    out_ref, sems = refs[-2:]
    copies = []
    for s in range(4):
        source = (own_ref, far_ref)[s // 2]
        start = pl.multiple_of(at_ref[s] * STEP, STEP)
        copies.append(
            pltpu.make_async_copy(
                source.at[:, pl.ds((s % 2) * STEP, STEP)],
                out_ref.at[:, pl.ds(start, STEP)],
                sems.at[s],
            )
        )
    for copy in copies:
        copy.start()
    for copy in copies:
        copy.wait()


def place(at, own, far, columns, out):
    rows = own.shape[0]
    anywhere = pl.BlockSpec(memory_space=pl.ANY)
    operands = [at, own, far] + ([] if out is None else [out])
    return pl.pallas_call(
        place_kernel,
        in_specs=[pl.BlockSpec(memory_space=pltpu.SMEM)]
        + [anywhere] * (len(operands) - 1),
        out_specs=anywhere,
        out_shape=jax.ShapeDtypeStruct((rows, columns), F32),
        scratch_shapes=[pltpu.SemaphoreType.DMA((4,))],
        input_output_aliases={} if out is None else {3: 0},
        cost_estimate=pl.CostEstimate(
            flops=0, bytes_accessed=8 * rows * STEP * 4, transcendentals=0
        ),
        name="place",
    )(*operands)


def local_pair(library, annulus):
    rows = library.shape[0]
    frames = lax.axis_size("frame")
    frame = lax.axis_index("frame")
    x = lax.axis_index("pix")
    z = frame // 4

    def swap_x(a):
        return lax.ppermute(a, "pix", [(0, 1), (1, 0)])

    def swap_y(a):
        return lax.ppermute(a, "frame", [(f, f ^ 2) for f in range(frames)])

    def swap_core(a):
        return lax.ppermute(a, "frame", [(f, f ^ 1) for f in range(frames)])

    def next_z(a):
        return lax.ppermute(a, "frame", [(f, (f + 4) % frames) for f in range(frames)])

    pieces = pick(library, annulus)

    ring = [pieces]
    for _ in range(3):
        ring.append([next_z(a) for a in ring[-1]])

    other = [swap_x(a) for a in pieces]
    near = unit_rows(pieces, other)
    far = unit_rows([swap_y(a) for a in pieces], [swap_y(a) for a in other])

    out = None
    for j in range(2):
        first_here = ((z - j) % 4) // 2 == x
        at = jnp.stack(
            [
                (((z - j) % 2) * 4 + ((frame % 4) ^ s)) * (rows // STEP)
                for s in range(4)
            ]
        ).astype(jnp.int32)
        columns = []
        for k in range(len(pieces)):
            a, b = ring[j][k], ring[j + 2][k]
            keep = jnp.where(first_here, a, b)
            received = swap_x(jnp.where(first_here, b, a))
            columns.append([keep, received, swap_core(keep), swap_core(received)])
        for k, blocks in enumerate(columns):
            own, sent = product(k, near, far, blocks, columns[0])
            out = place(at + k, own, swap_y(sent), frames // 2 * rows, out)
    return out


def local(library, annulus):
    picked = jnp.take(library, annulus, axis=1)
    total = lax.psum(jnp.sum(picked, axis=1), "pix")
    frame_mean = total / PIX
    centered = picked - frame_mean[:, None]
    squares = lax.psum(jnp.sum(centered * centered, axis=1), "pix")
    unit = centered / jnp.sqrt(squares + EPS)[:, None]
    partial_gram = lax.dot_general(
        unit,
        lax.all_gather(unit, "frame", axis=0, tiled=True),
        (((1,), (1,)), ((), ())),
        precision=lax.Precision.HIGHEST,
        preferred_element_type=jnp.float32,
    )
    return lax.psum_scatter(partial_gram, "pix", scatter_dimension=1, tiled=True)


def solution(mesh):
    placed = (P("frame", "pix"), P("pix"))
    pair = mesh.shape["pix"] == 2 and mesh.shape["frame"] == 16
    return jax.shard_map(
        local_pair if pair else local,
        mesh=mesh, in_specs=placed, out_specs=P("frame", "pix"), check_vma=False,
    )
```

```python
import functools

import jax
import jax.numpy as jnp
from jax import lax
from jax.experimental import pallas as pl
from jax.experimental.pallas import tpu as pltpu
from jax.sharding import PartitionSpec as P

PIX = 1536
EPS = 1e-06
CHUNKS = (128, 128, 128)
STAT_ROWS = 8
VMEM = 28 << 20
F32, BF16 = jnp.float32, jnp.bfloat16


def split(a):
    high = a.astype(BF16)
    return high, (a - high.astype(F32)).astype(BF16)


def pick_kernel(annulus_ref, library_ref, whole_ref, *piece_refs):
    rows, band = library_ref.shape
    pix = annulus_ref.shape[1]
    tile = 256
    width = band - pix + tile
    columns = []
    for start in range(0, pix, tile):
        a = library_ref[:, start : start + width]
        high, rest = split(a)
        mid, low = split(a - high.astype(F32))
        where = annulus_ref[:, start : start + tile] - start
        one_hot = jnp.where(
            lax.broadcasted_iota(jnp.int32, (width, tile), 0) == where, 1.0, 0.0
        ).astype(BF16)
        parts = jnp.dot(
            jnp.concatenate([high, mid, low], axis=0),
            one_hot,
            preferred_element_type=F32,
        )
        columns.append(
            parts[:rows] + parts[rows : 2 * rows] + parts[2 * rows :]
        )
    picked = jnp.concatenate(columns, axis=1)
    mean = jnp.sum(picked, axis=1, keepdims=True) / pix
    centered = picked - mean
    shift = jnp.sum(centered, axis=1, keepdims=True) / pix
    centered = centered - shift
    mean = mean + shift
    squares = jnp.sum(centered * centered, axis=1, keepdims=True)
    as_row = [
        jnp.transpose(jnp.broadcast_to(v, (rows, 128)))[:STAT_ROWS]
        for v in (mean, squares)
    ]
    stat = jnp.concatenate(as_row, axis=1)
    whole_ref[:rows], whole_ref[rows:] = centered, stat
    start = 0
    for ref, count in zip(piece_refs, CHUNKS):
        ref[:count] = centered[start : start + count]
        start += count
    piece_refs[0][CHUNKS[0] :] = stat


def pick(library, annulus):
    rows = library.shape[0]
    pix = annulus.shape[0]
    counts = [rows + STAT_ROWS, CHUNKS[0] + STAT_ROWS, *CHUNKS[1:]]
    return pl.pallas_call(
        pick_kernel,
        out_shape=[jax.ShapeDtypeStruct((count, pix), F32) for count in counts],
        compiler_params=pltpu.CompilerParams(vmem_limit_bytes=VMEM),
        name="pick",
    )(annulus.reshape(1, pix), library)


def gate_kernel(*refs):
    pass


def gate(arrays, after):
    n = len(arrays)
    return pl.pallas_call(
        gate_kernel,
        in_specs=[pl.BlockSpec(memory_space=pl.ANY)] * (n + len(after)),
        out_specs=[pl.BlockSpec(memory_space=pl.ANY)] * n,
        out_shape=[jax.ShapeDtypeStruct(a.shape, a.dtype) for a in arrays],
        input_output_aliases={i: i for i in range(n)},
        name="gate",
    )(*arrays, *after)


def choose_kernel(first_ref, a_ref, b_ref, *refs):
    keep_ref, send_ref = refs[-2:]
    first = first_ref[0] == 1
    a, b = a_ref[...], b_ref[...]
    keep_ref[...] = jnp.where(first, a, b)
    send_ref[...] = jnp.where(first, b, a)


def choose(first, a, b, after):
    vmem = pl.BlockSpec(memory_space=pltpu.VMEM)
    return pl.pallas_call(
        choose_kernel,
        in_specs=[pl.BlockSpec(memory_space=pltpu.SMEM), vmem, vmem]
        + [pl.BlockSpec(memory_space=pl.ANY)] * len(after),
        out_specs=[vmem] * 2,
        out_shape=[jax.ShapeDtypeStruct(a.shape, a.dtype)] * 2,
        compiler_params=pltpu.CompilerParams(vmem_limit_bytes=VMEM),
        name="choose",
    )(first, a, b, *after)


def pair_kernel(a_ref, b_ref, *refs):
    refs[-1][0], refs[-1][1] = a_ref[...], b_ref[...]


def pair(a, b, after):
    vmem = pl.BlockSpec(memory_space=pltpu.VMEM)
    return pl.pallas_call(
        pair_kernel,
        in_specs=[vmem] * 2 + [pl.BlockSpec(memory_space=pl.ANY)] * len(after),
        out_specs=vmem,
        out_shape=jax.ShapeDtypeStruct((2,) + a.shape, a.dtype),
        compiler_params=pltpu.CompilerParams(vmem_limit_bytes=VMEM),
        name="pair",
    )(a, b, *after)


def normalize(a, b, a_stat, b_stat, start):
    count, pix = a.shape
    rows = a_stat.shape[1] // 2
    mean = slice(start, start + count)
    squares = slice(rows + start, rows + start + count)
    gap = (a_stat[:, mean] - b_stat[:, mean]) / 2
    total = a_stat[:, squares] + b_stat[:, squares] + (2 * pix) * (gap * gap)
    scale = 1 / jnp.sqrt(total + EPS)
    gap, scale = [
        jnp.transpose(jnp.broadcast_to(v, (128, count)))[:, :1] for v in (gap, scale)
    ]
    return jnp.concatenate([(a + gap) * scale, (b - gap) * scale], axis=1)


def rows_kernel(a_ref, b_ref, out_ref):
    rows = a_ref.shape[0] - STAT_ROWS
    unit = normalize(
        a_ref[:rows], b_ref[:rows], a_ref[rows : rows + 1], b_ref[rows : rows + 1], 0
    )
    out_ref[:rows], out_ref[rows:] = split(unit)


def unit_rows(a, b):
    rows, pix = a.shape[0] - STAT_ROWS, a.shape[1]
    return pl.pallas_call(
        rows_kernel,
        out_shape=jax.ShapeDtypeStruct((2 * rows, 2 * pix), BF16),
        compiler_params=pltpu.CompilerParams(vmem_limit_bytes=VMEM),
        cost_estimate=pl.CostEstimate(
            flops=6 * rows * pix, bytes_accessed=16 * rows * pix, transcendentals=0
        ),
        name="unit_rows",
    )(a, b)


def product_kernel(start, count, *refs):
    rows_refs, refs = refs[:2], refs[2:]
    keep, received, pair = refs[:3]
    columns = [keep[...], received[...], pair[0], pair[1]]
    if start == 0:
        stats = [a[count : count + 1] for a in columns]
    else:
        stats = [refs[3][0:1], refs[4][0:1], refs[5][0, 0:1], refs[5][1, 0:1]]
    outs = refs[-2:]
    unit = jnp.concatenate(
        [
            normalize(
                columns[c][:count], columns[c + 1][:count], stats[c], stats[c + 1], start
            )
            for c in (0, 2)
        ],
        axis=0,
    )
    high, low = split(unit)
    dot = functools.partial(
        lax.dot_general,
        dimension_numbers=(((1,), (1,)), ((), ())),
        preferred_element_type=F32,
    )
    for rows_ref, out_ref in zip(rows_refs, outs):
        rows = rows_ref.shape[0] // 2
        both = dot(rows_ref[...], high)
        out_ref[...] = both[:rows] + (both[rows:] + dot(rows_ref[:rows], low))


def product(i, near, far, columns, first):
    double, depth = near.shape
    start, count = sum(CHUNKS[:i]), CHUNKS[i]
    vmem = pl.BlockSpec(memory_space=pltpu.VMEM)
    in_specs = [vmem] * 5
    operands = [near, far, *columns]
    if i:
        at, pix = CHUNKS[0] // STAT_ROWS, depth // 2
        in_specs += [pl.BlockSpec((STAT_ROWS, pix), lambda i: (at, 0))] * 2
        in_specs.append(pl.BlockSpec((2, STAT_ROWS, pix), lambda i: (0, at, 0)))
        operands += first
    out = jax.ShapeDtypeStruct((double // 2, 2 * count), F32)
    return pl.pallas_call(
        functools.partial(product_kernel, start, count),
        grid=(1,),
        in_specs=in_specs,
        out_specs=[vmem] * 2,
        out_shape=[out] * 2,
        compiler_params=pltpu.CompilerParams(vmem_limit_bytes=VMEM),
        cost_estimate=pl.CostEstimate(
            flops=6 * double * 2 * count * depth,
            bytes_accessed=4 * double * depth + 4 * double * 2 * count,
            transcendentals=0,
        ),
        name="product",
    )(*operands)


def place_kernel(at_ref, *refs):
    out_ref = refs[-1]
    n = len(CHUNKS)
    for side in range(2):

        @pl.when(pl.program_id(0) // 2 == side)
        def _():
            out_ref[...] = jnp.concatenate(
                [ref[...] for ref in refs[side * n : side * n + n]], axis=1
            )


def place(at, own, far, frames, out):
    rows = own[0].shape[0]
    in_specs = [
        pl.BlockSpec((rows, count), lambda i, at: (0, i % 2)) for count in CHUNKS
    ] * 2
    operands = [at, *own, *far]
    alias = {}
    if out is not None:
        in_specs.append(pl.BlockSpec(memory_space=pl.ANY))
        alias = {len(operands): 0}
        operands.append(out)
    return pl.pallas_call(
        place_kernel,
        grid_spec=pltpu.PrefetchScalarGridSpec(
            num_scalar_prefetch=1,
            grid=(4,),
            in_specs=in_specs,
            out_specs=pl.BlockSpec((rows, rows), lambda i, at: (0, at[i])),
        ),
        out_shape=jax.ShapeDtypeStruct((rows, frames * rows), F32),
        input_output_aliases=alias,
        compiler_params=pltpu.CompilerParams(vmem_limit_bytes=VMEM),
        cost_estimate=pl.CostEstimate(
            flops=0, bytes_accessed=32 * rows * rows, transcendentals=0
        ),
        name="place",
    )(*operands)


def local_pair(library, annulus):
    frames = lax.axis_size("frame")
    frame = lax.axis_index("frame")
    x = lax.axis_index("pix")
    z = frame // 4

    def swap_x(a):
        return lax.ppermute(a, "pix", [(0, 1), (1, 0)])

    def swap_y(a):
        return lax.ppermute(a, "frame", [(f, f ^ 2) for f in range(frames)])

    def swap_core(a):
        return lax.ppermute(a, "frame", [(f, f ^ 1) for f in range(frames)])

    def next_z(a):
        return lax.ppermute(a, "frame", [(f, (f + 4) % frames) for f in range(frames)])

    whole, *chunks = pick(library, annulus)

    other, far = swap_x(whole), swap_y(whole)
    ring = [chunks, gate([next_z(a) for a in chunks], [other, far])]
    for _ in range(2):
        ring.append([next_z(a) for a in ring[-1]])

    far_other = swap_y(other)
    near = unit_rows(whole, other)
    far = unit_rows(far, far_other)

    out = None
    swapped = []
    for j in range(2):
        first = (((z - j) % 4) // 2 == x).astype(jnp.int32).reshape(1)
        at = jnp.stack([((z - j) % 2) * 4 + ((frame % 4) ^ s) for s in range(4)])
        if j == 0:
            before_choose = [[], [], [far_other]]
            before_pair = [[], [], ring[3][:1]]
        else:
            before_choose = [[sent], swapped[:1], swapped[1:2]]
            before_pair = [ring[3][1:2], ring[3][2:3], swapped[2:3]]
        columns, owns, swaps = [], [], []
        for i, (a, b) in enumerate(zip(ring[j], ring[j + 2])):
            keep, send = choose(first, a, b, before_choose[i])
            received = swap_x(send)
            both = swap_core(pair(keep, received, before_pair[i]))
            columns.append([keep, received, both])
            own, sent_now = product(i, near, far, columns[i], columns[0])
            if i == 0:
                sent = sent_now
            owns.append(own)
            swaps.append(swap_y(sent_now))
        swapped = swaps
        out = place(at.astype(jnp.int32), owns, swaps, frames // 2, out)
    return out


def local(library, annulus):
    picked = jnp.take(library, annulus, axis=1)
    total = lax.psum(jnp.sum(picked, axis=1), "pix")
    frame_mean = total / PIX
    centered = picked - frame_mean[:, None]
    squares = lax.psum(jnp.sum(centered * centered, axis=1), "pix")
    unit = centered / jnp.sqrt(squares + EPS)[:, None]
    partial_gram = lax.dot_general(
        unit,
        lax.all_gather(unit, "frame", axis=0, tiled=True),
        (((1,), (1,)), ((), ())),
        precision=lax.Precision.HIGHEST,
        preferred_element_type=jnp.float32,
    )
    return lax.psum_scatter(partial_gram, "pix", scatter_dimension=1, tiled=True)


def solution(mesh):
    placed = (P("frame", "pix"), P("pix"))
    pair = mesh.shape["pix"] == 2 and mesh.shape["frame"] == 16
    return jax.shard_map(
        local_pair if pair else local,
        mesh=mesh, in_specs=placed, out_specs=P("frame", "pix"), check_vma=False,
    )
```

```python
import functools

import jax
import jax.numpy as jnp
from jax import lax
from jax.experimental import pallas as pl
from jax.experimental.pallas import tpu as pltpu
from jax.sharding import PartitionSpec as P

PIX = 1536
EPS = 1e-06
CHUNKS = (128, 128, 128)
STAT_ROWS = 8
SMALL, VMEM = 6 << 20, 28 << 20
FREE = pl.CostEstimate(flops=1, bytes_accessed=1, transcendentals=0)
F32, BF16 = jnp.float32, jnp.bfloat16


def split(a):
    high = a.astype(BF16)
    return high, (a - high.astype(F32)).astype(BF16)


def pick_kernel(annulus_ref, library_ref, whole_ref, *piece_refs):
    rows, band = library_ref.shape
    pix = annulus_ref.shape[1]
    tile = 256
    width = band - pix + tile
    columns = []
    for start in range(0, pix, tile):
        a = library_ref[:, start : start + width]
        high, rest = split(a)
        mid, low = split(a - high.astype(F32))
        where = annulus_ref[:, start : start + tile] - start
        one_hot = jnp.where(
            lax.broadcasted_iota(jnp.int32, (width, tile), 0) == where, 1.0, 0.0
        ).astype(BF16)
        parts = jnp.dot(
            jnp.concatenate([high, mid, low], axis=0),
            one_hot,
            preferred_element_type=F32,
        )
        columns.append(
            parts[:rows] + parts[rows : 2 * rows] + parts[2 * rows :]
        )
    picked = jnp.concatenate(columns, axis=1)
    mean = jnp.sum(picked, axis=1, keepdims=True) / pix
    centered = picked - mean
    shift = jnp.sum(centered, axis=1, keepdims=True) / pix
    centered = centered - shift
    mean = mean + shift
    squares = jnp.sum(centered * centered, axis=1, keepdims=True)
    as_row = [
        jnp.transpose(jnp.broadcast_to(v, (rows, 128)))[:STAT_ROWS]
        for v in (mean, squares)
    ]
    stat = jnp.concatenate(as_row, axis=1)
    whole_ref[:rows], whole_ref[rows:] = centered, stat
    start = 0
    for ref, count in zip(piece_refs, CHUNKS):
        ref[:count] = centered[start : start + count]
        start += count
    piece_refs[0][CHUNKS[0] :] = stat


def pick(library, annulus):
    rows = library.shape[0]
    pix = annulus.shape[0]
    counts = [rows + STAT_ROWS, CHUNKS[0] + STAT_ROWS, *CHUNKS[1:]]
    return pl.pallas_call(
        pick_kernel,
        out_shape=[jax.ShapeDtypeStruct((count, pix), F32) for count in counts],
        compiler_params=pltpu.CompilerParams(vmem_limit_bytes=VMEM),
        cost_estimate=FREE,
        name="pick",
    )(annulus.reshape(1, pix), library)


def cut_kernel(whole_ref, *refs):
    out_refs = refs[-len(CHUNKS) :]
    rows = whole_ref.shape[0] - STAT_ROWS
    start = 0
    for ref, count in zip(out_refs, CHUNKS):
        ref[:count] = whole_ref[start : start + count]
        start += count
    out_refs[0][CHUNKS[0] :] = whole_ref[rows:]


def cut(whole, after):
    pix = whole.shape[1]
    counts = [CHUNKS[0] + STAT_ROWS, *CHUNKS[1:]]
    vmem = pl.BlockSpec(memory_space=pltpu.VMEM)
    return pl.pallas_call(
        cut_kernel,
        in_specs=[vmem] + [pl.BlockSpec(memory_space=pl.ANY)] * len(after),
        out_specs=[vmem] * len(counts),
        out_shape=[jax.ShapeDtypeStruct((count, pix), F32) for count in counts],
        compiler_params=pltpu.CompilerParams(vmem_limit_bytes=SMALL),
        cost_estimate=FREE,
        name="cut",
    )(whole, *after)


def choose_kernel(first_ref, a_ref, b_ref, *refs):
    keep_ref, send_ref = refs[-2:]
    first = first_ref[0] == 1
    a, b = a_ref[...], b_ref[...]
    keep_ref[...] = jnp.where(first, a, b)
    send_ref[...] = jnp.where(first, b, a)


def choose(first, a, b, after):
    vmem = pl.BlockSpec(memory_space=pltpu.VMEM)
    return pl.pallas_call(
        choose_kernel,
        in_specs=[pl.BlockSpec(memory_space=pltpu.SMEM), vmem, vmem]
        + [pl.BlockSpec(memory_space=pl.ANY)] * len(after),
        out_specs=[vmem] * 2,
        out_shape=[jax.ShapeDtypeStruct(a.shape, a.dtype)] * 2,
        compiler_params=pltpu.CompilerParams(vmem_limit_bytes=SMALL),
        cost_estimate=FREE,
        name="choose",
    )(first, a, b, *after)


def pair_kernel(a_ref, b_ref, *refs):
    refs[-1][0], refs[-1][1] = a_ref[...], b_ref[...]


def pair(a, b, after):
    vmem = pl.BlockSpec(memory_space=pltpu.VMEM)
    return pl.pallas_call(
        pair_kernel,
        in_specs=[vmem] * 2 + [pl.BlockSpec(memory_space=pl.ANY)] * len(after),
        out_specs=vmem,
        out_shape=jax.ShapeDtypeStruct((2,) + a.shape, a.dtype),
        compiler_params=pltpu.CompilerParams(vmem_limit_bytes=SMALL),
        cost_estimate=FREE,
        name="pair",
    )(a, b, *after)


def normalize(a, b, a_stat, b_stat, start):
    count, pix = a.shape
    rows = a_stat.shape[1] // 2
    mean = slice(start, start + count)
    squares = slice(rows + start, rows + start + count)
    gap = (a_stat[:, mean] - b_stat[:, mean]) / 2
    total = a_stat[:, squares] + b_stat[:, squares] + (2 * pix) * (gap * gap)
    scale = 1 / jnp.sqrt(total + EPS)
    gap, scale = [
        jnp.transpose(jnp.broadcast_to(v, (128, count)))[:, :1] for v in (gap, scale)
    ]
    return jnp.concatenate([(a + gap) * scale, (b - gap) * scale], axis=1)


def rows_kernel(a_ref, b_ref, out_ref):
    rows = a_ref.shape[0] - STAT_ROWS
    unit = normalize(
        a_ref[:rows], b_ref[:rows], a_ref[rows : rows + 1], b_ref[rows : rows + 1], 0
    )
    out_ref[:rows], out_ref[rows:] = split(unit)


def unit_rows(a, b):
    rows, pix = a.shape[0] - STAT_ROWS, a.shape[1]
    return pl.pallas_call(
        rows_kernel,
        out_shape=jax.ShapeDtypeStruct((2 * rows, 2 * pix), BF16),
        compiler_params=pltpu.CompilerParams(vmem_limit_bytes=VMEM),
        cost_estimate=FREE,
        name="unit_rows",
    )(a, b)


def product_kernel(start, count, *refs):
    rows_refs, refs = refs[:2], refs[2:]
    keep, received, pair = refs[:3]
    columns = [keep[...], received[...], pair[0], pair[1]]
    if start == 0:
        stats = [a[count : count + 1] for a in columns]
    else:
        stats = [refs[3][0:1], refs[4][0:1], refs[5][0, 0:1], refs[5][1, 0:1]]
    outs = refs[-2:]
    unit = jnp.concatenate(
        [
            normalize(
                columns[c][:count], columns[c + 1][:count], stats[c], stats[c + 1], start
            )
            for c in (0, 2)
        ],
        axis=0,
    )
    high, low = split(unit)
    dot = functools.partial(
        lax.dot_general,
        dimension_numbers=(((1,), (1,)), ((), ())),
        preferred_element_type=F32,
    )
    for rows_ref, out_ref in zip(rows_refs, outs):
        rows = rows_ref.shape[0] // 2
        both = dot(rows_ref[...], high)
        out_ref[...] = both[:rows] + (both[rows:] + dot(rows_ref[:rows], low))


def product(i, near, far, columns, first):
    double, depth = near.shape
    start, count = sum(CHUNKS[:i]), CHUNKS[i]
    vmem = pl.BlockSpec(memory_space=pltpu.VMEM)
    in_specs = [vmem] * 5
    operands = [near, far, *columns]
    if i:
        at, pix = CHUNKS[0] // STAT_ROWS, depth // 2
        in_specs += [pl.BlockSpec((STAT_ROWS, pix), lambda i: (at, 0))] * 2
        in_specs.append(pl.BlockSpec((2, STAT_ROWS, pix), lambda i: (0, at, 0)))
        operands += first
    out = jax.ShapeDtypeStruct((double // 2, 2 * count), F32)
    return pl.pallas_call(
        functools.partial(product_kernel, start, count),
        grid=(1,),
        in_specs=in_specs,
        out_specs=[vmem] * 2,
        out_shape=[out] * 2,
        compiler_params=pltpu.CompilerParams(vmem_limit_bytes=VMEM),
        cost_estimate=FREE,
        name="product",
    )(*operands)


def place_kernel(at_ref, *refs):
    out_ref = refs[-1]
    n = len(CHUNKS)
    for side in range(2):

        @pl.when(pl.program_id(0) // 2 == side)
        def _():
            out_ref[...] = jnp.concatenate(
                [ref[...] for ref in refs[side * n : side * n + n]], axis=1
            )


def place(at, own, far, frames, out):
    rows = own[0].shape[0]
    in_specs = [
        pl.BlockSpec((rows, count), lambda i, at: (0, i % 2)) for count in CHUNKS
    ] * 2
    operands = [at, *own, *far]
    alias = {}
    if out is not None:
        in_specs.append(pl.BlockSpec(memory_space=pl.ANY))
        alias = {len(operands): 0}
        operands.append(out)
    return pl.pallas_call(
        place_kernel,
        grid_spec=pltpu.PrefetchScalarGridSpec(
            num_scalar_prefetch=1,
            grid=(4,),
            in_specs=in_specs,
            out_specs=pl.BlockSpec((rows, rows), lambda i, at: (0, at[i])),
        ),
        out_shape=jax.ShapeDtypeStruct((rows, frames * rows), F32),
        input_output_aliases=alias,
        compiler_params=pltpu.CompilerParams(vmem_limit_bytes=VMEM),
        cost_estimate=FREE,
        name="place",
    )(*operands)


def local_pair(library, annulus):
    frames = lax.axis_size("frame")
    frame = lax.axis_index("frame")
    x = lax.axis_index("pix")
    z = frame // 4

    def swap_x(a):
        return lax.ppermute(a, "pix", [(0, 1), (1, 0)])

    def swap_y(a):
        return lax.ppermute(a, "frame", [(f, f ^ 2) for f in range(frames)])

    def swap_core(a):
        return lax.ppermute(a, "frame", [(f, f ^ 1) for f in range(frames)])

    def next_z(a):
        return lax.ppermute(a, "frame", [(f, (f + 4) % frames) for f in range(frames)])

    whole, *chunks = pick(library, annulus)

    other, far = swap_x(whole), swap_y(whole)
    ring = [chunks, cut(next_z(whole), [other, far])]
    for _ in range(2):
        ring.append([next_z(a) for a in ring[-1]])

    far_other = swap_y(other)
    near = unit_rows(whole, other)
    far = unit_rows(far, far_other)

    out = None
    swapped = []
    for j in range(2):
        first = (((z - j) % 4) // 2 == x).astype(jnp.int32).reshape(1)
        at = jnp.stack([((z - j) % 2) * 4 + ((frame % 4) ^ s) for s in range(4)])
        if j == 0:
            before_choose = [[],[],[far_other]]
            before_pair = [[],ring[3][:1],ring[3][1:2]]
        else:
            before_choose = [sent[:1],swapped[:1]+ring[3][2:3],swapped[1:2]]
            before_pair = [[],[],swapped[2:3]]
        columns, owns, swaps, sents = [], [], [], []
        for i, (a, b) in enumerate(zip(ring[j], ring[j + 2])):
            keep, send = choose(first, a, b, before_choose[i])
            received = swap_x(send)
            both = swap_core(pair(keep, received, before_pair[i]))
            columns.append([keep, received, both])
            own, sent_now = product(i, near, far, columns[i], columns[0])
            sents.append(sent_now)
            owns.append(own)
            swaps.append(swap_y(sent_now))
        swapped, sent = swaps, sents
        out = place(at.astype(jnp.int32), owns, swaps, frames // 2, out)
    return out


def local(library, annulus):
    picked = jnp.take(library, annulus, axis=1)
    total = lax.psum(jnp.sum(picked, axis=1), "pix")
    frame_mean = total / PIX
    centered = picked - frame_mean[:, None]
    squares = lax.psum(jnp.sum(centered * centered, axis=1), "pix")
    unit = centered / jnp.sqrt(squares + EPS)[:, None]
    partial_gram = lax.dot_general(
        unit,
        lax.all_gather(unit, "frame", axis=0, tiled=True),
        (((1,), (1,)), ((), ())),
        precision=lax.Precision.HIGHEST,
        preferred_element_type=jnp.float32,
    )
    return lax.psum_scatter(partial_gram, "pix", scatter_dimension=1, tiled=True)


def solution(mesh):
    placed = (P("frame", "pix"), P("pix"))
    pair = mesh.shape["pix"] == 2 and mesh.shape["frame"] == 16
    return jax.shard_map(
        local_pair if pair else local,
        mesh=mesh, in_specs=placed, out_specs=P("frame", "pix"), check_vma=False,
    )
```

```python
import functools

import jax
import jax.numpy as jnp
from jax import lax
from jax.experimental import pallas as pl
from jax.experimental.pallas import tpu as pltpu
from jax.sharding import PartitionSpec as P

PIX = 1536
EPS = 1e-06
CHUNKS = (128, 128, 128)
STAT_ROWS = 8
SMALL, VMEM = 6 << 20, 28 << 20
FREE = pl.CostEstimate(flops=1, bytes_accessed=1, transcendentals=0)
F32, BF16 = jnp.float32, jnp.bfloat16


def split(a):
    high = a.astype(BF16)
    return high, (a - high.astype(F32)).astype(BF16)


def pick_kernel(annulus_ref, library_ref, whole_ref, *piece_refs):
    rows, band = library_ref.shape
    pix = annulus_ref.shape[1]
    tile = 256
    width = band - pix + tile
    columns = []
    for start in range(0, pix, tile):
        a = library_ref[:, start : start + width]
        high, rest = split(a)
        mid, low = split(a - high.astype(F32))
        where = annulus_ref[:, start : start + tile] - start
        one_hot = jnp.where(
            lax.broadcasted_iota(jnp.int32, (width, tile), 0) == where, 1.0, 0.0
        ).astype(BF16)
        parts = jnp.dot(
            jnp.concatenate([high, mid, low], axis=0),
            one_hot,
            preferred_element_type=F32,
        )
        columns.append(
            parts[:rows] + parts[rows : 2 * rows] + parts[2 * rows :]
        )
    picked = jnp.concatenate(columns, axis=1)
    mean = jnp.sum(picked, axis=1, keepdims=True) / pix
    centered = picked - mean
    shift = jnp.sum(centered, axis=1, keepdims=True) / pix
    centered = centered - shift
    mean = mean + shift
    squares = jnp.sum(centered * centered, axis=1, keepdims=True)
    as_row = [
        jnp.transpose(jnp.broadcast_to(v, (rows, 128)))[:STAT_ROWS]
        for v in (mean, squares)
    ]
    stat = jnp.concatenate(as_row, axis=1)
    whole_ref[:rows], whole_ref[rows:] = centered, stat
    start = 0
    for ref, count in zip(piece_refs, CHUNKS):
        ref[:count] = centered[start : start + count]
        start += count
    piece_refs[0][CHUNKS[0] :] = stat


def pick(library, annulus):
    rows = library.shape[0]
    pix = annulus.shape[0]
    counts = [rows + STAT_ROWS, CHUNKS[0] + STAT_ROWS, *CHUNKS[1:]]
    return pl.pallas_call(
        pick_kernel,
        out_shape=[jax.ShapeDtypeStruct((count, pix), F32) for count in counts],
        compiler_params=pltpu.CompilerParams(vmem_limit_bytes=VMEM),
        cost_estimate=FREE,
        name="pick",
    )(annulus.reshape(1, pix), library)


def cut_kernel(whole_ref, *refs):
    out_refs = refs[-len(CHUNKS) :]
    rows = whole_ref.shape[0] - STAT_ROWS
    start = 0
    for ref, count in zip(out_refs, CHUNKS):
        ref[:count] = whole_ref[start : start + count]
        start += count
    out_refs[0][CHUNKS[0] :] = whole_ref[rows:]


def cut(whole, after):
    pix = whole.shape[1]
    counts = [CHUNKS[0] + STAT_ROWS, *CHUNKS[1:]]
    vmem = pl.BlockSpec(memory_space=pltpu.VMEM)
    return pl.pallas_call(
        cut_kernel,
        in_specs=[vmem] + [pl.BlockSpec(memory_space=pl.ANY)] * len(after),
        out_specs=[vmem] * len(counts),
        out_shape=[jax.ShapeDtypeStruct((count, pix), F32) for count in counts],
        compiler_params=pltpu.CompilerParams(vmem_limit_bytes=SMALL),
        cost_estimate=FREE,
        name="cut",
    )(whole, *after)


def choose_kernel(first_ref, a_ref, b_ref, *refs):
    keep_ref, send_ref = refs[-2:]
    first = first_ref[0] == 1
    a, b = a_ref[...], b_ref[...]
    keep_ref[...] = jnp.where(first, a, b)
    send_ref[...] = jnp.where(first, b, a)


def choose(first, a, b, after):
    vmem = pl.BlockSpec(memory_space=pltpu.VMEM)
    return pl.pallas_call(
        choose_kernel,
        in_specs=[pl.BlockSpec(memory_space=pltpu.SMEM), vmem, vmem]
        + [pl.BlockSpec(memory_space=pl.ANY)] * len(after),
        out_specs=[vmem] * 2,
        out_shape=[jax.ShapeDtypeStruct(a.shape, a.dtype)] * 2,
        compiler_params=pltpu.CompilerParams(vmem_limit_bytes=SMALL),
        cost_estimate=FREE,
        name="choose",
    )(first, a, b, *after)


def pair_kernel(a_ref, b_ref, *refs):
    refs[-1][0], refs[-1][1] = a_ref[...], b_ref[...]


def pair(a, b, after):
    vmem = pl.BlockSpec(memory_space=pltpu.VMEM)
    return pl.pallas_call(
        pair_kernel,
        in_specs=[vmem] * 2 + [pl.BlockSpec(memory_space=pl.ANY)] * len(after),
        out_specs=vmem,
        out_shape=jax.ShapeDtypeStruct((2,) + a.shape, a.dtype),
        compiler_params=pltpu.CompilerParams(vmem_limit_bytes=SMALL),
        cost_estimate=FREE,
        name="pair",
    )(a, b, *after)


def normalize(a, b, a_stat, b_stat, start):
    count, pix = a.shape
    rows = a_stat.shape[1] // 2
    mean = slice(start, start + count)
    squares = slice(rows + start, rows + start + count)
    gap = (a_stat[:, mean] - b_stat[:, mean]) / 2
    total = a_stat[:, squares] + b_stat[:, squares] + (2 * pix) * (gap * gap)
    scale = 1 / jnp.sqrt(total + EPS)
    gap, scale = [
        jnp.transpose(jnp.broadcast_to(v, (128, count)))[:, :1] for v in (gap, scale)
    ]
    return jnp.concatenate([(a + gap) * scale, (b - gap) * scale], axis=1)


def rows_kernel(a_ref, b_ref, out_ref):
    rows = a_ref.shape[0] - STAT_ROWS
    unit = normalize(
        a_ref[:rows], b_ref[:rows], a_ref[rows : rows + 1], b_ref[rows : rows + 1], 0
    )
    out_ref[:rows], out_ref[rows:] = split(unit)


def unit_rows(a, b):
    rows, pix = a.shape[0] - STAT_ROWS, a.shape[1]
    return pl.pallas_call(
        rows_kernel,
        out_shape=jax.ShapeDtypeStruct((2 * rows, 2 * pix), BF16),
        compiler_params=pltpu.CompilerParams(vmem_limit_bytes=VMEM),
        cost_estimate=FREE,
        name="unit_rows",
    )(a, b)


def product_kernel(start, count, *refs):
    rows_refs, refs = refs[:2], refs[2:]
    keep, received, pair = refs[:3]
    columns = [keep[...], received[...], pair[0], pair[1]]
    if start == 0:
        stats = [a[count : count + 1] for a in columns]
    else:
        stats = [refs[3][0:1], refs[4][0:1], refs[5][0, 0:1], refs[5][1, 0:1]]
    outs = refs[-2:]
    unit = jnp.concatenate(
        [
            normalize(
                columns[c][:count], columns[c + 1][:count], stats[c], stats[c + 1], start
            )
            for c in (0, 2)
        ],
        axis=0,
    )
    high, low = split(unit)
    dot = functools.partial(
        lax.dot_general,
        dimension_numbers=(((1,), (1,)), ((), ())),
        preferred_element_type=F32,
    )
    for rows_ref, out_ref in zip(rows_refs, outs):
        rows = rows_ref.shape[0] // 2
        both = dot(rows_ref[...], high)
        out_ref[...] = both[:rows] + (both[rows:] + dot(rows_ref[:rows], low))


def product(i, near, far, columns, first, after):
    double, depth = near.shape
    start, count = sum(CHUNKS[:i]), CHUNKS[i]
    vmem = pl.BlockSpec(memory_space=pltpu.VMEM)
    in_specs = [vmem] * 5
    operands = [near, far, *columns]
    if i:
        at, pix = CHUNKS[0] // STAT_ROWS, depth // 2
        in_specs += [pl.BlockSpec((STAT_ROWS, pix), lambda i: (at, 0))] * 2
        in_specs.append(pl.BlockSpec((2, STAT_ROWS, pix), lambda i: (0, at, 0)))
        operands += first
    in_specs += [pl.BlockSpec(memory_space=pl.ANY)] * len(after)
    operands += after
    out = jax.ShapeDtypeStruct((double // 2, 2 * count), F32)
    return pl.pallas_call(
        functools.partial(product_kernel, start, count),
        grid=(1,),
        in_specs=in_specs,
        out_specs=[vmem] * 2,
        out_shape=[out] * 2,
        compiler_params=pltpu.CompilerParams(vmem_limit_bytes=VMEM),
        cost_estimate=FREE,
        name="product",
    )(*operands)


def place_kernel(at_ref, *refs):
    out_ref = refs[-1]
    n = len(CHUNKS)
    for side in range(2):

        @pl.when(pl.program_id(0) // 2 == side)
        def _():
            out_ref[...] = jnp.concatenate(
                [ref[...] for ref in refs[side * n : side * n + n]], axis=1
            )


def place(at, own, far, frames, out):
    rows = own[0].shape[0]
    in_specs = [
        pl.BlockSpec((rows, count), lambda i, at: (0, i % 2)) for count in CHUNKS
    ] * 2
    operands = [at, *own, *far]
    alias = {}
    if out is not None:
        in_specs.append(pl.BlockSpec(memory_space=pl.ANY))
        alias = {len(operands): 0}
        operands.append(out)
    return pl.pallas_call(
        place_kernel,
        grid_spec=pltpu.PrefetchScalarGridSpec(
            num_scalar_prefetch=1,
            grid=(4,),
            in_specs=in_specs,
            out_specs=pl.BlockSpec((rows, rows), lambda i, at: (0, at[i])),
        ),
        out_shape=jax.ShapeDtypeStruct((rows, frames * rows), F32),
        input_output_aliases=alias,
        compiler_params=pltpu.CompilerParams(vmem_limit_bytes=VMEM),
        cost_estimate=FREE,
        name="place",
    )(*operands)


def local_pair(library, annulus):
    frames = lax.axis_size("frame")
    frame = lax.axis_index("frame")
    x = lax.axis_index("pix")
    z = frame // 4

    def swap_x(a):
        return lax.ppermute(a, "pix", [(0, 1), (1, 0)])

    def swap_y(a):
        return lax.ppermute(a, "frame", [(f, f ^ 2) for f in range(frames)])

    def swap_core(a):
        return lax.ppermute(a, "frame", [(f, f ^ 1) for f in range(frames)])

    def next_z(a):
        return lax.ppermute(a, "frame", [(f, (f + 4) % frames) for f in range(frames)])

    whole, *chunks = pick(library, annulus)

    other, far = swap_x(whole), swap_y(whole)
    ring = [chunks, cut(next_z(whole), [other, far])]
    for _ in range(2):
        ring.append([next_z(a) for a in ring[-1]])

    far_other = swap_y(other)
    near = unit_rows(whole, other)
    far = unit_rows(far, far_other)

    first = [(((z - j) % 4) // 2 == x).astype(jnp.int32).reshape(1) for j in range(2)]
    keep, chosen, received, paired, columns = {}, {}, {}, {}, {}
    own, sent, back = {}, {}, {}

    def send(j, k, *after):
        keep[j, k], chosen[j, k] = choose(first[j], ring[j][k], ring[j + 2][k], after)
        received[j, k] = swap_x(chosen[j, k])

    def share(j, k, *after):
        paired[j, k] = pair(keep[j, k], received[j, k], after)
        columns[j, k] = [keep[j, k], received[j, k], swap_core(paired[j, k])]

    def multiply(j, k, *after):
        own[j, k], sent[j, k] = product(k, near, far, columns[j, k], columns[j, 0], after)
        back[j, k] = swap_y(sent[j, k])

    send(0, 0)
    send(0, 1)
    share(0, 0)
    multiply(0, 0)
    share(0, 1, far_other)
    send(0, 2)
    multiply(0, 1)
    share(0, 2, sent[0, 0], far_other)
    multiply(0, 2)
    send(1, 0)
    send(1, 1, sent[0, 1], back[0, 0])
    send(1, 2, sent[0, 2])
    share(1, 0, back[0, 0])
    multiply(1, 0)
    share(1, 1, back[0, 1])
    multiply(1, 1, sent[0, 0])
    share(1, 2, back[0, 2])
    multiply(1, 2)
    out = None
    for j in range(2):
        at = jnp.stack([((z - j) % 2) * 4 + ((frame % 4) ^ s) for s in range(4)])
        out = place(
            at.astype(jnp.int32),
            [own[j, k] for k in range(len(CHUNKS))],
            [back[j, k] for k in range(len(CHUNKS))],
            frames // 2,
            out,
        )
    return out


def local(library, annulus):
    picked = jnp.take(library, annulus, axis=1)
    total = lax.psum(jnp.sum(picked, axis=1), "pix")
    frame_mean = total / PIX
    centered = picked - frame_mean[:, None]
    squares = lax.psum(jnp.sum(centered * centered, axis=1), "pix")
    unit = centered / jnp.sqrt(squares + EPS)[:, None]
    partial_gram = lax.dot_general(
        unit,
        lax.all_gather(unit, "frame", axis=0, tiled=True),
        (((1,), (1,)), ((), ())),
        precision=lax.Precision.HIGHEST,
        preferred_element_type=jnp.float32,
    )
    return lax.psum_scatter(partial_gram, "pix", scatter_dimension=1, tiled=True)


def solution(mesh):
    placed = (P("frame", "pix"), P("pix"))
    pair = mesh.shape["pix"] == 2 and mesh.shape["frame"] == 16
    return jax.shard_map(
        local_pair if pair else local,
        mesh=mesh, in_specs=placed, out_specs=P("frame", "pix"), check_vma=False,
    )
```

```python
import functools

import jax
import jax.numpy as jnp
from jax import lax
from jax.experimental import pallas as pl
from jax.experimental.pallas import tpu as pltpu
from jax.sharding import PartitionSpec as P

PIX = 1536
EPS = 1e-06
CHUNKS = (128, 128, 128)
STAT_ROWS = 8
SMALL, VMEM = 6 << 20, 28 << 20
FREE = pl.CostEstimate(flops=1, bytes_accessed=1, transcendentals=0)
F32, BF16 = jnp.float32, jnp.bfloat16


def split(a):
    high = a.astype(BF16)
    return high, (a - high.astype(F32)).astype(BF16)


def pick_kernel(annulus_ref, library_ref, place_ref, whole_ref, *piece_refs):
    rows, band = library_ref.shape
    pix = annulus_ref.shape[0]
    frame, x = lax.axis_index("frame"), lax.axis_index("pix")
    z = frame // 4
    for j in range(2):
        place_ref[j] = jnp.where((z + 4 - j) % 4 // 2 == x, 1, 0)
        for s in range(4):
            place_ref[2 + 4 * j + s] = (z + 4 - j) % 2 * 4 + ((frame % 4) ^ s)
    tile = 256
    width = band - pix + tile
    columns = []
    for start in range(0, pix, tile):
        a = library_ref[:, start : start + width]
        high, rest = split(a)
        mid, low = split(a - high.astype(F32))
        where = annulus_ref[start : start + tile].reshape(1, tile) - start
        one_hot = jnp.where(
            lax.broadcasted_iota(jnp.int32, (width, tile), 0) == where, 1.0, 0.0
        ).astype(BF16)
        parts = jnp.dot(
            jnp.concatenate([high, mid, low], axis=0),
            one_hot,
            preferred_element_type=F32,
        )
        columns.append(
            parts[:rows] + parts[rows : 2 * rows] + parts[2 * rows :]
        )
    picked = jnp.concatenate(columns, axis=1)
    mean = jnp.sum(picked, axis=1, keepdims=True) / pix
    centered = picked - mean
    shift = jnp.sum(centered, axis=1, keepdims=True) / pix
    centered = centered - shift
    mean = mean + shift
    squares = jnp.sum(centered * centered, axis=1, keepdims=True)
    as_row = [
        jnp.transpose(jnp.broadcast_to(v, (rows, 128)))[:STAT_ROWS]
        for v in (mean, squares)
    ]
    stat = jnp.concatenate(as_row, axis=1)
    whole_ref[:rows], whole_ref[rows:] = centered, stat
    start = 0
    for ref, count in zip(piece_refs, CHUNKS):
        ref[:count] = centered[start : start + count]
        start += count
    piece_refs[0][CHUNKS[0] :] = stat


def pick(library, annulus):
    rows = library.shape[0]
    pix = annulus.shape[0]
    counts = [rows + STAT_ROWS, CHUNKS[0] + STAT_ROWS, *CHUNKS[1:]]
    return pl.pallas_call(
        pick_kernel,
        out_shape=[jax.ShapeDtypeStruct((10,), jnp.int32)]
        + [jax.ShapeDtypeStruct((count, pix), F32) for count in counts],
        out_specs=[pl.BlockSpec(memory_space=pltpu.SMEM)]
        + [pl.BlockSpec(memory_space=pltpu.VMEM)] * len(counts),
        compiler_params=pltpu.CompilerParams(vmem_limit_bytes=VMEM),
        cost_estimate=FREE,
        name="pick",
    )(annulus, library)


def cut_kernel(whole_ref, *refs):
    out_refs = refs[-len(CHUNKS) :]
    rows = whole_ref.shape[0] - STAT_ROWS
    start = 0
    for ref, count in zip(out_refs, CHUNKS):
        ref[:count] = whole_ref[start : start + count]
        start += count
    out_refs[0][CHUNKS[0] :] = whole_ref[rows:]


def cut(whole, after):
    pix = whole.shape[1]
    counts = [CHUNKS[0] + STAT_ROWS, *CHUNKS[1:]]
    vmem = pl.BlockSpec(memory_space=pltpu.VMEM)
    return pl.pallas_call(
        cut_kernel,
        in_specs=[vmem] + [pl.BlockSpec(memory_space=pl.ANY)] * len(after),
        out_specs=[vmem] * len(counts),
        out_shape=[jax.ShapeDtypeStruct((count, pix), F32) for count in counts],
        compiler_params=pltpu.CompilerParams(vmem_limit_bytes=SMALL),
        cost_estimate=FREE,
        name="cut",
    )(whole, *after)


def choose_kernel(j, first_ref, a_ref, b_ref, *refs):
    keep_ref, send_ref = refs[-2:]
    first = first_ref[j] == 1
    a, b = a_ref[...], b_ref[...]
    keep_ref[...] = jnp.where(first, a, b)
    send_ref[...] = jnp.where(first, b, a)


def choose(j, spots, a, b, after):
    vmem = pl.BlockSpec(memory_space=pltpu.VMEM)
    return pl.pallas_call(
        functools.partial(choose_kernel, j),
        in_specs=[pl.BlockSpec(memory_space=pltpu.SMEM), vmem, vmem]
        + [pl.BlockSpec(memory_space=pl.ANY)] * len(after),
        out_specs=[vmem] * 2,
        out_shape=[jax.ShapeDtypeStruct(a.shape, a.dtype)] * 2,
        compiler_params=pltpu.CompilerParams(vmem_limit_bytes=SMALL),
        cost_estimate=FREE,
        name="choose",
    )(spots, a, b, *after)


def pair_kernel(a_ref, b_ref, *refs):
    refs[-1][0], refs[-1][1] = a_ref[...], b_ref[...]


def pair(a, b, after):
    vmem = pl.BlockSpec(memory_space=pltpu.VMEM)
    return pl.pallas_call(
        pair_kernel,
        in_specs=[vmem] * 2 + [pl.BlockSpec(memory_space=pl.ANY)] * len(after),
        out_specs=vmem,
        out_shape=jax.ShapeDtypeStruct((2,) + a.shape, a.dtype),
        compiler_params=pltpu.CompilerParams(vmem_limit_bytes=SMALL),
        cost_estimate=FREE,
        name="pair",
    )(a, b, *after)


def normalize(a, b, a_stat, b_stat, start):
    count, pix = a.shape
    rows = a_stat.shape[1] // 2
    mean = slice(start, start + count)
    squares = slice(rows + start, rows + start + count)
    gap = (a_stat[:, mean] - b_stat[:, mean]) / 2
    total = a_stat[:, squares] + b_stat[:, squares] + (2 * pix) * (gap * gap)
    scale = 1 / jnp.sqrt(total + EPS)
    gap, scale = [
        jnp.transpose(jnp.broadcast_to(v, (128, count)))[:, :1] for v in (gap, scale)
    ]
    return jnp.concatenate([(a + gap) * scale, (b - gap) * scale], axis=1)


def rows_kernel(a_ref, b_ref, out_ref):
    rows = a_ref.shape[0] - STAT_ROWS
    unit = normalize(
        a_ref[:rows], b_ref[:rows], a_ref[rows : rows + 1], b_ref[rows : rows + 1], 0
    )
    out_ref[:rows], out_ref[rows:] = split(unit)


def unit_rows(a, b):
    rows, pix = a.shape[0] - STAT_ROWS, a.shape[1]
    return pl.pallas_call(
        rows_kernel,
        out_shape=jax.ShapeDtypeStruct((2 * rows, 2 * pix), BF16),
        compiler_params=pltpu.CompilerParams(vmem_limit_bytes=VMEM),
        cost_estimate=FREE,
        name="unit_rows",
    )(a, b)


def product_kernel(start, count, *refs):
    rows_refs, refs = refs[:2], refs[2:]
    keep, received, pair = refs[:3]
    columns = [keep[...], received[...], pair[0], pair[1]]
    if start == 0:
        stats = [a[count : count + 1] for a in columns]
    else:
        stats = [refs[3][0:1], refs[4][0:1], refs[5][0, 0:1], refs[5][1, 0:1]]
    outs = refs[-2:]
    unit = jnp.concatenate(
        [
            normalize(
                columns[c][:count], columns[c + 1][:count], stats[c], stats[c + 1], start
            )
            for c in (0, 2)
        ],
        axis=0,
    )
    high, low = split(unit)
    dot = functools.partial(
        lax.dot_general,
        dimension_numbers=(((1,), (1,)), ((), ())),
        preferred_element_type=F32,
    )
    for rows_ref, out_ref in zip(rows_refs, outs):
        rows = rows_ref.shape[0] // 2
        both = dot(rows_ref[...], high)
        out_ref[...] = both[:rows] + (both[rows:] + dot(rows_ref[:rows], low))


def product(i, near, far, columns, first, after):
    double, depth = near.shape
    start, count = sum(CHUNKS[:i]), CHUNKS[i]
    vmem = pl.BlockSpec(memory_space=pltpu.VMEM)
    in_specs = [vmem] * 5
    operands = [near, far, *columns]
    if i:
        at, pix = CHUNKS[0] // STAT_ROWS, depth // 2
        in_specs += [pl.BlockSpec((STAT_ROWS, pix), lambda i: (at, 0))] * 2
        in_specs.append(pl.BlockSpec((2, STAT_ROWS, pix), lambda i: (0, at, 0)))
        operands += first
    in_specs += [pl.BlockSpec(memory_space=pl.ANY)] * len(after)
    operands += after
    out = jax.ShapeDtypeStruct((double // 2, 2 * count), F32)
    return pl.pallas_call(
        functools.partial(product_kernel, start, count),
        grid=(1,),
        in_specs=in_specs,
        out_specs=[vmem] * 2,
        out_shape=[out] * 2,
        compiler_params=pltpu.CompilerParams(vmem_limit_bytes=VMEM),
        cost_estimate=FREE,
        name="product",
    )(*operands)


def place_kernel(at_ref, *refs):
    out_ref = refs[-1]
    n = len(CHUNKS)
    for side in range(2):

        @pl.when(pl.program_id(0) // 2 == side)
        def _():
            out_ref[...] = jnp.concatenate(
                [ref[...] for ref in refs[side * n : side * n + n]], axis=1
            )


def place(j, spots, own, far, frames, out):
    rows = own[0].shape[0]
    in_specs = [
        pl.BlockSpec((rows, count), lambda i, at: (0, i % 2)) for count in CHUNKS
    ] * 2
    operands = [spots, *own, *far]
    alias = {}
    if out is not None:
        in_specs.append(pl.BlockSpec(memory_space=pl.ANY))
        alias = {len(operands): 0}
        operands.append(out)
    return pl.pallas_call(
        place_kernel,
        grid_spec=pltpu.PrefetchScalarGridSpec(
            num_scalar_prefetch=1,
            grid=(4,),
            in_specs=in_specs,
            out_specs=pl.BlockSpec((rows, rows), lambda i, at: (0, at[2 + 4 * j + i])),
        ),
        out_shape=jax.ShapeDtypeStruct((rows, frames * rows), F32),
        input_output_aliases=alias,
        compiler_params=pltpu.CompilerParams(vmem_limit_bytes=VMEM),
        cost_estimate=FREE,
        name="place",
    )(*operands)


def local_pair(library, annulus):
    frames = lax.axis_size("frame")

    def swap_x(a):
        return lax.ppermute(a, "pix", [(0, 1), (1, 0)])

    def swap_y(a):
        return lax.ppermute(a, "frame", [(f, f ^ 2) for f in range(frames)])

    def swap_core(a):
        return lax.ppermute(a, "frame", [(f, f ^ 1) for f in range(frames)])

    def next_z(a):
        return lax.ppermute(a, "frame", [(f, (f + 4) % frames) for f in range(frames)])

    spots, whole, *chunks = pick(library, annulus)

    other, far = swap_x(whole), swap_y(whole)
    ring = [chunks, cut(next_z(whole), [other, far])]
    for _ in range(2):
        ring.append([next_z(a) for a in ring[-1]])

    far_other = swap_y(other)
    near = unit_rows(whole, other)
    far = unit_rows(far, far_other)

    keep, chosen, received, paired, columns = {}, {}, {}, {}, {}
    own, sent, back = {}, {}, {}

    def send(j, k, *after):
        keep[j, k], chosen[j, k] = choose(j, spots, ring[j][k], ring[j + 2][k], after)
        received[j, k] = swap_x(chosen[j, k])

    def share(j, k, *after):
        paired[j, k] = pair(keep[j, k], received[j, k], after)
        columns[j, k] = [keep[j, k], received[j, k], swap_core(paired[j, k])]

    def multiply(j, k, *after):
        own[j, k], sent[j, k] = product(k, near, far, columns[j, k], columns[j, 0], after)
        back[j, k] = swap_y(sent[j, k])

    send(0, 0)
    send(0, 1)
    share(0, 0)
    multiply(0, 0)
    share(0, 1, far_other)
    send(0, 2)
    multiply(0, 1)
    share(0, 2, sent[0, 0], far_other)
    multiply(0, 2)
    send(1, 0)
    send(1, 1, sent[0, 1], back[0, 0])
    send(1, 2, sent[0, 2])
    share(1, 0, back[0, 0])
    multiply(1, 0)
    share(1, 1, back[0, 1])
    multiply(1, 1, sent[0, 0])
    share(1, 2, back[0, 2])
    multiply(1, 2)
    out = None
    for j in range(2):
        out = place(
            j,
            spots,
            [own[j, k] for k in range(len(CHUNKS))],
            [back[j, k] for k in range(len(CHUNKS))],
            frames // 2,
            out,
        )
    return out


def local(library, annulus):
    picked = jnp.take(library, annulus, axis=1)
    total = lax.psum(jnp.sum(picked, axis=1), "pix")
    frame_mean = total / PIX
    centered = picked - frame_mean[:, None]
    squares = lax.psum(jnp.sum(centered * centered, axis=1), "pix")
    unit = centered / jnp.sqrt(squares + EPS)[:, None]
    partial_gram = lax.dot_general(
        unit,
        lax.all_gather(unit, "frame", axis=0, tiled=True),
        (((1,), (1,)), ((), ())),
        precision=lax.Precision.HIGHEST,
        preferred_element_type=jnp.float32,
    )
    return lax.psum_scatter(partial_gram, "pix", scatter_dimension=1, tiled=True)


def solution(mesh):
    placed = (P("frame", "pix"), P("pix"))
    pair = mesh.shape["pix"] == 2 and mesh.shape["frame"] == 16
    return jax.shard_map(
        local_pair if pair else local,
        mesh=mesh, in_specs=placed, out_specs=P("frame", "pix"), check_vma=False,
    )
```

```python
import functools

import jax
import jax.numpy as jnp
from jax import lax
from jax.experimental import pallas as pl
from jax.experimental.pallas import tpu as pltpu
from jax.sharding import PartitionSpec as P

PIX = 1536
EPS = 1e-06
CHUNKS = (128, 128, 128)
STAT_ROWS = 8
SMALL, VMEM = 6 << 20, 28 << 20
FREE = pl.CostEstimate(flops=1, bytes_accessed=1, transcendentals=0)
F32, BF16 = jnp.float32, jnp.bfloat16


def split(a):
    high = a.astype(BF16)
    return high, (a - high.astype(F32)).astype(BF16)


def pick_kernel(annulus_hbm, library_hbm, place_ref, whole_ref, *refs):
    piece_refs, (annulus_ref, library_ref, sems) = refs[:-3], refs[-3:]
    rows, band = library_ref.shape
    pix = annulus_ref.shape[0]
    spans = [slice(sum(CHUNKS[:i]), sum(CHUNKS[: i + 1])) for i in range(len(CHUNKS))]
    copies = [pltpu.make_async_copy(annulus_hbm, annulus_ref, sems.at[0])]
    for i, span in enumerate(spans):
        copies.append(
            pltpu.make_async_copy(
                library_hbm.at[span], library_ref.at[span], sems.at[1 + i]
            )
        )
    for copy in copies:
        copy.start()

    frame, x = lax.axis_index("frame"), lax.axis_index("pix")
    z = frame // 4
    for j in range(2):
        place_ref[j] = jnp.where((z + 4 - j) % 4 // 2 == x, 1, 0)
        for s in range(4):
            place_ref[2 + 4 * j + s] = (z + 4 - j) % 2 * 4 + ((frame % 4) ^ s)

    copies[0].wait()
    tile = 256
    width = band - pix + tile
    one_hots = []
    for start in range(0, pix, tile):
        where = annulus_ref[start : start + tile].reshape(1, tile) - start
        at = lax.broadcasted_iota(jnp.int32, (width, tile), 0)
        one_hots.append(jnp.where(at == where, 1.0, 0.0).astype(BF16))
    for i, span in enumerate(spans):
        copies[1 + i].wait()
        count = CHUNKS[i]
        columns = []
        for t, one_hot in enumerate(one_hots):
            a = library_ref[span, t * tile : t * tile + width]
            high, rest = split(a)
            mid, low = split(a - high.astype(F32))
            parts = jnp.dot(
                jnp.concatenate([high, mid, low], axis=0),
                one_hot,
                preferred_element_type=F32,
            )
            columns.append(
                parts[:count] + parts[count : 2 * count] + parts[2 * count :]
            )
        picked = jnp.concatenate(columns, axis=1)
        mean = jnp.sum(picked, axis=1, keepdims=True) / pix
        centered = picked - mean
        shift = jnp.sum(centered, axis=1, keepdims=True) / pix
        centered = centered - shift
        mean = mean + shift
        squares = jnp.sum(centered * centered, axis=1, keepdims=True)
        whole_ref[span] = centered
        piece_refs[i][:count] = centered
        for start, v in ((0, mean), (rows, squares)):
            as_row = jnp.transpose(jnp.broadcast_to(v, (count, 128)))[:STAT_ROWS]
            lanes = slice(start + span.start, start + span.stop)
            whole_ref[rows:, lanes] = as_row
            piece_refs[0][CHUNKS[0] :, lanes] = as_row


def pick(library, annulus):
    rows = library.shape[0]
    pix = annulus.shape[0]
    counts = [rows + STAT_ROWS, CHUNKS[0] + STAT_ROWS, *CHUNKS[1:]]
    return pl.pallas_call(
        pick_kernel,
        out_shape=[jax.ShapeDtypeStruct((10,), jnp.int32)]
        + [jax.ShapeDtypeStruct((count, pix), F32) for count in counts],
        out_specs=[pl.BlockSpec(memory_space=pltpu.SMEM)]
        + [pl.BlockSpec(memory_space=pltpu.VMEM)] * len(counts),
        in_specs=[pl.BlockSpec(memory_space=pl.ANY)] * 2,
        scratch_shapes=[
            pltpu.VMEM(annulus.shape, jnp.int32),
            pltpu.VMEM(library.shape, F32),
            pltpu.SemaphoreType.DMA((1 + len(CHUNKS),)),
        ],
        compiler_params=pltpu.CompilerParams(vmem_limit_bytes=VMEM),
        cost_estimate=FREE,
        name="pick",
    )(annulus, library)


def cut_kernel(whole_ref, *refs):
    out_refs = refs[-len(CHUNKS) :]
    rows = whole_ref.shape[0] - STAT_ROWS
    start = 0
    for ref, count in zip(out_refs, CHUNKS):
        ref[:count] = whole_ref[start : start + count]
        start += count
    out_refs[0][CHUNKS[0] :] = whole_ref[rows:]


def cut(whole, after):
    pix = whole.shape[1]
    counts = [CHUNKS[0] + STAT_ROWS, *CHUNKS[1:]]
    vmem = pl.BlockSpec(memory_space=pltpu.VMEM)
    return pl.pallas_call(
        cut_kernel,
        in_specs=[vmem] + [pl.BlockSpec(memory_space=pl.ANY)] * len(after),
        out_specs=[vmem] * len(counts),
        out_shape=[jax.ShapeDtypeStruct((count, pix), F32) for count in counts],
        compiler_params=pltpu.CompilerParams(vmem_limit_bytes=SMALL),
        cost_estimate=FREE,
        name="cut",
    )(whole, *after)


def choose_kernel(j, first_ref, a_ref, b_ref, *refs):
    keep_ref, send_ref = refs[-2:]
    first = first_ref[j] == 1
    a, b = a_ref[...], b_ref[...]
    keep_ref[...] = jnp.where(first, a, b)
    send_ref[...] = jnp.where(first, b, a)


def choose(j, spots, a, b, after):
    vmem = pl.BlockSpec(memory_space=pltpu.VMEM)
    return pl.pallas_call(
        functools.partial(choose_kernel, j),
        in_specs=[pl.BlockSpec(memory_space=pltpu.SMEM), vmem, vmem]
        + [pl.BlockSpec(memory_space=pl.ANY)] * len(after),
        out_specs=[vmem] * 2,
        out_shape=[jax.ShapeDtypeStruct(a.shape, a.dtype)] * 2,
        compiler_params=pltpu.CompilerParams(vmem_limit_bytes=SMALL),
        cost_estimate=FREE,
        name="choose",
    )(spots, a, b, *after)


def pair_kernel(a_ref, b_ref, *refs):
    refs[-1][0], refs[-1][1] = a_ref[...], b_ref[...]


def pair(a, b, after):
    vmem = pl.BlockSpec(memory_space=pltpu.VMEM)
    return pl.pallas_call(
        pair_kernel,
        in_specs=[vmem] * 2 + [pl.BlockSpec(memory_space=pl.ANY)] * len(after),
        out_specs=vmem,
        out_shape=jax.ShapeDtypeStruct((2,) + a.shape, a.dtype),
        compiler_params=pltpu.CompilerParams(vmem_limit_bytes=SMALL),
        cost_estimate=FREE,
        name="pair",
    )(a, b, *after)


def normalize(a, b, a_stat, b_stat, start):
    count, pix = a.shape
    rows = a_stat.shape[1] // 2
    mean = slice(start, start + count)
    squares = slice(rows + start, rows + start + count)
    gap = (a_stat[:, mean] - b_stat[:, mean]) / 2
    total = a_stat[:, squares] + b_stat[:, squares] + (2 * pix) * (gap * gap)
    scale = 1 / jnp.sqrt(total + EPS)
    gap, scale = [
        jnp.transpose(jnp.broadcast_to(v, (128, count)))[:, :1] for v in (gap, scale)
    ]
    return jnp.concatenate([(a + gap) * scale, (b - gap) * scale], axis=1)


def rows_kernel(a_ref, b_ref, out_ref):
    rows = a_ref.shape[0] - STAT_ROWS
    unit = normalize(
        a_ref[:rows], b_ref[:rows], a_ref[rows : rows + 1], b_ref[rows : rows + 1], 0
    )
    out_ref[:rows], out_ref[rows:] = split(unit)


def unit_rows(a, b):
    rows, pix = a.shape[0] - STAT_ROWS, a.shape[1]
    return pl.pallas_call(
        rows_kernel,
        out_shape=jax.ShapeDtypeStruct((2 * rows, 2 * pix), BF16),
        compiler_params=pltpu.CompilerParams(vmem_limit_bytes=12 << 20),
        cost_estimate=FREE,
        name="unit_rows",
    )(a, b)


def product_kernel(start, count, *refs):
    rows_refs, refs = refs[:2], refs[2:]
    keep, received, pair = refs[:3]
    columns = [keep[...], received[...], pair[0], pair[1]]
    if start == 0:
        stats = [a[count : count + 1] for a in columns]
    else:
        stats = [refs[3][0:1], refs[4][0:1], refs[5][0, 0:1], refs[5][1, 0:1]]
    outs = refs[-2:]
    unit = jnp.concatenate(
        [
            normalize(
                columns[c][:count], columns[c + 1][:count], stats[c], stats[c + 1], start
            )
            for c in (0, 2)
        ],
        axis=0,
    )
    high, low = split(unit)
    dot = functools.partial(
        lax.dot_general,
        dimension_numbers=(((1,), (1,)), ((), ())),
        preferred_element_type=F32,
    )
    for rows_ref, out_ref in zip(rows_refs, outs):
        rows = rows_ref.shape[0] // 2
        both = dot(rows_ref[...], high)
        out_ref[...] = both[:rows] + (both[rows:] + dot(rows_ref[:rows], low))


def product(i, near, far, columns, first, after):
    double, depth = near.shape
    start, count = sum(CHUNKS[:i]), CHUNKS[i]
    vmem = pl.BlockSpec(memory_space=pltpu.VMEM)
    in_specs = [vmem] * 5
    operands = [near, far, *columns]
    if i:
        at, pix = CHUNKS[0] // STAT_ROWS, depth // 2
        in_specs += [pl.BlockSpec((STAT_ROWS, pix), lambda i: (at, 0))] * 2
        in_specs.append(pl.BlockSpec((2, STAT_ROWS, pix), lambda i: (0, at, 0)))
        operands += first
    in_specs += [pl.BlockSpec(memory_space=pl.ANY)] * len(after)
    operands += after
    out = jax.ShapeDtypeStruct((double // 2, 2 * count), F32)
    return pl.pallas_call(
        functools.partial(product_kernel, start, count),
        grid=(1,),
        in_specs=in_specs,
        out_specs=[vmem] * 2,
        out_shape=[out] * 2,
        compiler_params=pltpu.CompilerParams(vmem_limit_bytes=16 << 20),
        cost_estimate=FREE,
        name="product",
    )(*operands)


def place_kernel(at_ref, *refs):
    out_ref = refs[-1]
    n = (len(refs) - 1) // 2
    for side in range(2):

        @pl.when(pl.program_id(0) // 2 == side)
        def _():
            parts = [ref[...] for ref in refs[side * n : side * n + n]]
            out_ref[...] = parts[0] if n == 1 else jnp.concatenate(parts, axis=1)


def place(j, k, spots, own, far, frames, out):
    rows = own[0].shape[0]
    counts = [a.shape[1] // 2 for a in own]
    width = sum(counts)
    in_specs = [pl.BlockSpec((rows, count), lambda i, at: (0, i % 2)) for count in counts]
    in_specs += in_specs
    operands = [spots, *own, *far]
    alias = {}
    if out is not None:
        in_specs.append(pl.BlockSpec(memory_space=pl.ANY))
        alias = {len(operands): 0}
        operands.append(out)
    return pl.pallas_call(
        place_kernel,
        grid_spec=pltpu.PrefetchScalarGridSpec(
            num_scalar_prefetch=1,
            grid=(4,),
            in_specs=in_specs,
            out_specs=pl.BlockSpec(
                (rows, width),
                lambda i, at: (0, at[2 + 4 * j + i] * (rows // width) + (k or 0)),
            ),
        ),
        out_shape=jax.ShapeDtypeStruct((rows, frames * rows), F32),
        input_output_aliases=alias,
        compiler_params=pltpu.CompilerParams(vmem_limit_bytes=10 << 20),
        cost_estimate=FREE,
        name="place",
    )(*operands)


def local_pair(library, annulus):
    frames = lax.axis_size("frame")

    def swap_x(a):
        return lax.ppermute(a, "pix", [(0, 1), (1, 0)])

    def swap_y(a):
        return lax.ppermute(a, "frame", [(f, f ^ 2) for f in range(frames)])

    def swap_core(a):
        return lax.ppermute(a, "frame", [(f, f ^ 1) for f in range(frames)])

    def next_z(a):
        return lax.ppermute(a, "frame", [(f, (f + 4) % frames) for f in range(frames)])

    spots, whole, *chunks = pick(library, annulus)

    other, far = swap_x(whole), swap_y(whole)
    ring = [chunks, cut(next_z(whole), [other, far])]
    for _ in range(2):
        ring.append([next_z(a) for a in ring[-1]])

    far_other = swap_y(other)
    near = unit_rows(whole, other)
    far = unit_rows(far, far_other)

    keep, chosen, received, paired, columns = {}, {}, {}, {}, {}
    own, sent, back = {}, {}, {}

    def send(j, k, *after):
        keep[j, k], chosen[j, k] = choose(j, spots, ring[j][k], ring[j + 2][k], after)
        received[j, k] = swap_x(chosen[j, k])

    def share(j, k, *after):
        paired[j, k] = pair(keep[j, k], received[j, k], after)
        columns[j, k] = [keep[j, k], received[j, k], swap_core(paired[j, k])]

    def multiply(j, k, *after):
        own[j, k], sent[j, k] = product(k, near, far, columns[j, k], columns[j, 0], after)
        back[j, k] = swap_y(sent[j, k])

    send(0, 0)
    send(0, 1)
    share(0, 0)
    multiply(0, 0)
    share(0, 1, far_other)
    send(0, 2)
    multiply(0, 1)
    share(0, 2, sent[0, 0], far_other)
    multiply(0, 2)
    send(1, 0)
    send(1, 1, sent[0, 1], back[0, 0], sent[0, 2])
    send(1, 2, sent[0, 2])
    share(1, 0, back[0, 0])
    multiply(1, 0)
    share(1, 1, back[0, 1])
    multiply(1, 1, sent[0, 0])
    share(1, 2, back[0, 2])
    multiply(1, 2)
    n = len(CHUNKS)
    out = place(
        0, None, spots, [own[0, k] for k in range(n)], [back[0, k] for k in range(n)],
        frames // 2, None,
    )
    for k in range(n):
        out = place(1, k, spots, [own[1, k]], [back[1, k]], frames // 2, out)
    return out


def local(library, annulus):
    picked = jnp.take(library, annulus, axis=1)
    total = lax.psum(jnp.sum(picked, axis=1), "pix")
    frame_mean = total / PIX
    centered = picked - frame_mean[:, None]
    squares = lax.psum(jnp.sum(centered * centered, axis=1), "pix")
    unit = centered / jnp.sqrt(squares + EPS)[:, None]
    partial_gram = lax.dot_general(
        unit,
        lax.all_gather(unit, "frame", axis=0, tiled=True),
        (((1,), (1,)), ((), ())),
        precision=lax.Precision.HIGHEST,
        preferred_element_type=jnp.float32,
    )
    return lax.psum_scatter(partial_gram, "pix", scatter_dimension=1, tiled=True)


def solution(mesh):
    placed = (P("frame", "pix"), P("pix"))
    pair = mesh.shape["pix"] == 2 and mesh.shape["frame"] == 16
    return jax.shard_map(
        local_pair if pair else local,
        mesh=mesh, in_specs=placed, out_specs=P("frame", "pix"), check_vma=False,
    )
```

```python
import functools

import jax
import jax.numpy as jnp
from jax import lax
from jax.experimental import pallas as pl
from jax.experimental.pallas import tpu as pltpu
from jax.sharding import PartitionSpec as P

PIX = 1536
EPS = 1e-06
CHUNKS = (128, 128, 128)
STAT_ROWS = 8
SMALL, VMEM = 6 << 20, 28 << 20
FREE = pl.CostEstimate(flops=1, bytes_accessed=1, transcendentals=0)
F32, BF16 = jnp.float32, jnp.bfloat16


def split(a):
    high = a.astype(BF16)
    return high, (a - high.astype(F32)).astype(BF16)


def pick_kernel(annulus_ref, library_ref, place_ref, whole_ref, *piece_refs):
    rows, band = library_ref.shape
    pix = annulus_ref.shape[0]
    frame, x = lax.axis_index("frame"), lax.axis_index("pix")
    z = frame // 4
    for j in range(2):
        place_ref[j] = jnp.where((z + 4 - j) % 4 // 2 == x, 1, 0)
        for s in range(4):
            place_ref[2 + 4 * j + s] = (z + 4 - j) % 2 * 4 + ((frame % 4) ^ s)
    tile = 256
    width = band - pix + tile
    columns = []
    for start in range(0, pix, tile):
        a = library_ref[:, start : start + width]
        high, rest = split(a)
        mid, low = split(a - high.astype(F32))
        where = annulus_ref[start : start + tile].reshape(1, tile) - start
        one_hot = jnp.where(
            lax.broadcasted_iota(jnp.int32, (width, tile), 0) == where, 1.0, 0.0
        ).astype(BF16)
        parts = jnp.dot(
            jnp.concatenate([high, mid, low], axis=0),
            one_hot,
            preferred_element_type=F32,
        )
        columns.append(
            parts[:rows] + parts[rows : 2 * rows] + parts[2 * rows :]
        )
    picked = jnp.concatenate(columns, axis=1)
    mean = jnp.sum(picked, axis=1, keepdims=True) / pix
    centered = picked - mean
    shift = jnp.sum(centered, axis=1, keepdims=True) / pix
    centered = centered - shift
    mean = mean + shift
    squares = jnp.sum(centered * centered, axis=1, keepdims=True)
    as_row = [
        jnp.transpose(jnp.broadcast_to(v, (rows, 128)))[:STAT_ROWS]
        for v in (mean, squares)
    ]
    stat = jnp.concatenate(as_row, axis=1)
    whole_ref[:rows], whole_ref[rows:] = centered, stat
    start = 0
    for ref, count in zip(piece_refs, CHUNKS):
        ref[:count] = centered[start : start + count]
        start += count
    piece_refs[0][CHUNKS[0] :] = stat


def pick(library, annulus):
    rows = library.shape[0]
    pix = annulus.shape[0]
    counts = [rows + STAT_ROWS, CHUNKS[0] + STAT_ROWS, *CHUNKS[1:]]
    return pl.pallas_call(
        pick_kernel,
        out_shape=[jax.ShapeDtypeStruct((10,), jnp.int32)]
        + [jax.ShapeDtypeStruct((count, pix), F32) for count in counts],
        out_specs=[pl.BlockSpec(memory_space=pltpu.SMEM)]
        + [pl.BlockSpec(memory_space=pltpu.VMEM)] * len(counts),
        compiler_params=pltpu.CompilerParams(vmem_limit_bytes=VMEM),
        cost_estimate=FREE,
        name="pick",
    )(annulus, library)


def cut_kernel(whole_ref, *refs):
    out_refs = refs[-len(CHUNKS) :]
    rows = whole_ref.shape[0] - STAT_ROWS
    start = 0
    for ref, count in zip(out_refs, CHUNKS):
        ref[:count] = whole_ref[start : start + count]
        start += count
    out_refs[0][CHUNKS[0] :] = whole_ref[rows:]


def cut(whole, after):
    pix = whole.shape[1]
    counts = [CHUNKS[0] + STAT_ROWS, *CHUNKS[1:]]
    vmem = pl.BlockSpec(memory_space=pltpu.VMEM)
    return pl.pallas_call(
        cut_kernel,
        in_specs=[vmem] + [pl.BlockSpec(memory_space=pl.ANY)] * len(after),
        out_specs=[vmem] * len(counts),
        out_shape=[jax.ShapeDtypeStruct((count, pix), F32) for count in counts],
        compiler_params=pltpu.CompilerParams(vmem_limit_bytes=SMALL),
        cost_estimate=FREE,
        name="cut",
    )(whole, *after)


def choose_kernel(j, first_ref, a_ref, b_ref, *refs):
    keep_ref, send_ref = refs[-2:]
    first = first_ref[j] == 1
    a, b = a_ref[...], b_ref[...]
    keep_ref[...] = jnp.where(first, a, b)
    send_ref[...] = jnp.where(first, b, a)


def choose(j, spots, a, b, after):
    vmem = pl.BlockSpec(memory_space=pltpu.VMEM)
    return pl.pallas_call(
        functools.partial(choose_kernel, j),
        in_specs=[pl.BlockSpec(memory_space=pltpu.SMEM), vmem, vmem]
        + [pl.BlockSpec(memory_space=pl.ANY)] * len(after),
        out_specs=[vmem] * 2,
        out_shape=[jax.ShapeDtypeStruct(a.shape, a.dtype)] * 2,
        compiler_params=pltpu.CompilerParams(vmem_limit_bytes=SMALL),
        cost_estimate=FREE,
        name="choose",
    )(spots, a, b, *after)


def pair_kernel(a_ref, b_ref, *refs):
    refs[-1][0], refs[-1][1] = a_ref[...], b_ref[...]


def pair(a, b, after):
    vmem = pl.BlockSpec(memory_space=pltpu.VMEM)
    return pl.pallas_call(
        pair_kernel,
        in_specs=[vmem] * 2 + [pl.BlockSpec(memory_space=pl.ANY)] * len(after),
        out_specs=vmem,
        out_shape=jax.ShapeDtypeStruct((2,) + a.shape, a.dtype),
        compiler_params=pltpu.CompilerParams(vmem_limit_bytes=SMALL),
        cost_estimate=FREE,
        name="pair",
    )(a, b, *after)


def normalize(a, b, a_stat, b_stat, start):
    count, pix = a.shape
    rows = a_stat.shape[1] // 2
    mean = slice(start, start + count)
    squares = slice(rows + start, rows + start + count)
    gap = (a_stat[:, mean] - b_stat[:, mean]) / 2
    total = a_stat[:, squares] + b_stat[:, squares] + (2 * pix) * (gap * gap)
    scale = 1 / jnp.sqrt(total + EPS)
    gap, scale = [
        jnp.transpose(jnp.broadcast_to(v, (128, count)))[:, :1] for v in (gap, scale)
    ]
    return jnp.concatenate([(a + gap) * scale, (b - gap) * scale], axis=1)


def rows_kernel(a_ref, b_ref, out_ref):
    rows = a_ref.shape[0] - STAT_ROWS
    unit = normalize(
        a_ref[:rows], b_ref[:rows], a_ref[rows : rows + 1], b_ref[rows : rows + 1], 0
    )
    out_ref[:rows], out_ref[rows:] = split(unit)


def unit_rows(a, b):
    rows, pix = a.shape[0] - STAT_ROWS, a.shape[1]
    return pl.pallas_call(
        rows_kernel,
        out_shape=jax.ShapeDtypeStruct((2 * rows, 2 * pix), BF16),
        compiler_params=pltpu.CompilerParams(vmem_limit_bytes=12 << 20),
        cost_estimate=FREE,
        name="unit_rows",
    )(a, b)


def product_kernel(start, count, *refs):
    rows_refs, refs = refs[:2], refs[2:]
    keep, received, pair = refs[:3]
    columns = [keep[...], received[...], pair[0], pair[1]]
    if start == 0:
        stats = [a[count : count + 1] for a in columns]
    else:
        stats = [refs[3][0:1], refs[4][0:1], refs[5][0, 0:1], refs[5][1, 0:1]]
    outs = refs[-2:]
    unit = jnp.concatenate(
        [
            normalize(
                columns[c][:count], columns[c + 1][:count], stats[c], stats[c + 1], start
            )
            for c in (0, 2)
        ],
        axis=0,
    )
    high, low = split(unit)
    dot = functools.partial(
        lax.dot_general,
        dimension_numbers=(((1,), (1,)), ((), ())),
        preferred_element_type=F32,
    )
    for rows_ref, out_ref in zip(rows_refs, outs):
        rows = rows_ref.shape[0] // 2
        both = dot(rows_ref[...], high)
        out_ref[...] = both[:rows] + (both[rows:] + dot(rows_ref[:rows], low))


def product(i, near, far, columns, first, after):
    double, depth = near.shape
    start, count = sum(CHUNKS[:i]), CHUNKS[i]
    vmem = pl.BlockSpec(memory_space=pltpu.VMEM)
    in_specs = [vmem] * 5
    operands = [near, far, *columns]
    if i:
        at, pix = CHUNKS[0] // STAT_ROWS, depth // 2
        in_specs += [pl.BlockSpec((STAT_ROWS, pix), lambda i: (at, 0))] * 2
        in_specs.append(pl.BlockSpec((2, STAT_ROWS, pix), lambda i: (0, at, 0)))
        operands += first
    in_specs += [pl.BlockSpec(memory_space=pl.ANY)] * len(after)
    operands += after
    out = jax.ShapeDtypeStruct((double // 2, 2 * count), F32)
    return pl.pallas_call(
        functools.partial(product_kernel, start, count),
        grid=(1,),
        in_specs=in_specs,
        out_specs=[vmem] * 2,
        out_shape=[out] * 2,
        compiler_params=pltpu.CompilerParams(vmem_limit_bytes=16 << 20),
        cost_estimate=FREE,
        name="product",
    )(*operands)


def place_kernel(at_ref, *refs):
    out_ref = refs[-1]
    n = (len(refs) - 1) // 2
    for side in range(2):

        @pl.when(pl.program_id(0) // 2 == side)
        def _():
            parts = [ref[...] for ref in refs[side * n : side * n + n]]
            out_ref[...] = parts[0] if n == 1 else jnp.concatenate(parts, axis=1)


def place(j, k, spots, own, far, frames, out):
    rows = own[0].shape[0]
    counts = [a.shape[1] // 2 for a in own]
    width = sum(counts)
    in_specs = [pl.BlockSpec((rows, count), lambda i, at: (0, i % 2)) for count in counts]
    in_specs += in_specs
    operands = [spots, *own, *far]
    alias = {}
    if out is not None:
        in_specs.append(pl.BlockSpec(memory_space=pl.ANY))
        alias = {len(operands): 0}
        operands.append(out)
    return pl.pallas_call(
        place_kernel,
        grid_spec=pltpu.PrefetchScalarGridSpec(
            num_scalar_prefetch=1,
            grid=(4,),
            in_specs=in_specs,
            out_specs=pl.BlockSpec(
                (rows, width),
                lambda i, at: (0, at[2 + 4 * j + i] * (rows // width) + (k or 0)),
            ),
        ),
        out_shape=jax.ShapeDtypeStruct((rows, frames * rows), F32),
        input_output_aliases=alias,
        compiler_params=pltpu.CompilerParams(vmem_limit_bytes=10 << 20),
        cost_estimate=FREE,
        name="place",
    )(*operands)


def local_pair(library, annulus):
    frames = lax.axis_size("frame")

    def swap_x(a):
        return lax.ppermute(a, "pix", [(0, 1), (1, 0)])

    def swap_y(a):
        return lax.ppermute(a, "frame", [(f, f ^ 2) for f in range(frames)])

    def swap_core(a):
        return lax.ppermute(a, "frame", [(f, f ^ 1) for f in range(frames)])

    def next_z(a):
        return lax.ppermute(a, "frame", [(f, (f + 4) % frames) for f in range(frames)])

    def previous_z(a):
        return lax.ppermute(a, "frame", [((f + 4) % frames, f) for f in range(frames)])

    spots, whole, *chunks = pick(library, annulus)

    other, far = swap_x(whole), swap_y(whole)
    ring = [chunks, cut(next_z(whole), [other, far])]
    ring.append([next_z(a) for a in ring[1]])
    ring.append([previous_z(a) for a in chunks])

    far_other = swap_y(other)
    near = unit_rows(whole, other)
    far = unit_rows(far, far_other)

    keep, chosen, received, paired, columns = {}, {}, {}, {}, {}
    own, sent, back = {}, {}, {}
    last = []

    def send(j, k, *after):
        keep[j, k], chosen[j, k] = choose(j, spots, ring[j][k], ring[j + 2][k], [*last, *after])
        received[j, k] = swap_x(chosen[j, k])
        last[:] = [chosen[j, k]]

    def share(j, k, *after):
        paired[j, k] = pair(keep[j, k], received[j, k], [*last, *after])
        columns[j, k] = [keep[j, k], received[j, k], swap_core(paired[j, k])]
        last[:] = [paired[j, k]]

    def multiply(j, k, *after):
        own[j, k], sent[j, k] = product(k, near, far, columns[j, k], columns[j, 0], [*last, *after])
        back[j, k] = swap_y(sent[j, k])
        last[:] = [sent[j, k]]

    send(0, 0)
    send(0, 1, far_other)
    share(0, 0)
    multiply(0, 0)
    send(0, 2)
    share(0, 1)
    multiply(0, 1)
    send(1, 0)
    share(0, 2, back[0, 0])
    multiply(0, 2)
    send(1, 1)
    share(1, 0, back[0, 1])
    multiply(1, 0)
    send(1, 2)
    share(1, 1, back[0, 2])
    multiply(1, 1)
    share(1, 2, back[1, 0])
    multiply(1, 2)
    n = len(CHUNKS)
    out = place(
        0, None, spots, [own[0, k] for k in range(n)], [back[0, k] for k in range(n)],
        frames // 2, None,
    )
    for k in range(n):
        out = place(1, k, spots, [own[1, k]], [back[1, k]], frames // 2, out)
    return out


def local(library, annulus):
    picked = jnp.take(library, annulus, axis=1)
    total = lax.psum(jnp.sum(picked, axis=1), "pix")
    frame_mean = total / PIX
    centered = picked - frame_mean[:, None]
    squares = lax.psum(jnp.sum(centered * centered, axis=1), "pix")
    unit = centered / jnp.sqrt(squares + EPS)[:, None]
    partial_gram = lax.dot_general(
        unit,
        lax.all_gather(unit, "frame", axis=0, tiled=True),
        (((1,), (1,)), ((), ())),
        precision=lax.Precision.HIGHEST,
        preferred_element_type=jnp.float32,
    )
    return lax.psum_scatter(partial_gram, "pix", scatter_dimension=1, tiled=True)


def solution(mesh):
    placed = (P("frame", "pix"), P("pix"))
    pair = mesh.shape["pix"] == 2 and mesh.shape["frame"] == 16
    return jax.shard_map(
        local_pair if pair else local,
        mesh=mesh, in_specs=placed, out_specs=P("frame", "pix"), check_vma=False,
    )
```

```python
import functools

import jax
import jax.numpy as jnp
from jax import lax
from jax.experimental import pallas as pl
from jax.experimental.pallas import tpu as pltpu
from jax.sharding import PartitionSpec as P

PIX = 1536
EPS = 1e-06
CHUNKS = (128, 128, 128)
STAT_ROWS = 8
SMALL, VMEM = 6 << 20, 28 << 20
FREE = pl.CostEstimate(flops=1, bytes_accessed=1, transcendentals=0)
F32, BF16 = jnp.float32, jnp.bfloat16


def split(a):
    high = a.astype(BF16)
    return high, (a - high.astype(F32)).astype(BF16)


def pick_kernel(annulus_ref, library_ref, place_ref, whole_ref, *piece_refs):
    rows, band = library_ref.shape
    pix = annulus_ref.shape[0]
    frame, x = lax.axis_index("frame"), lax.axis_index("pix")
    z = frame // 4
    for j in range(2):
        place_ref[j] = jnp.where((z + 4 - j) % 4 // 2 == x, 1, 0)
        for s in range(4):
            place_ref[2 + 4 * j + s] = (z + 4 - j) % 2 * 4 + ((frame % 4) ^ s)
    tile = 256
    width = band - pix + tile
    columns = []
    for start in range(0, pix, tile):
        a = library_ref[:, start : start + width]
        high, rest = split(a)
        mid, low = split(a - high.astype(F32))
        where = annulus_ref[start : start + tile].reshape(1, tile) - start
        one_hot = jnp.where(
            lax.broadcasted_iota(jnp.int32, (width, tile), 0) == where, 1.0, 0.0
        ).astype(BF16)
        parts = jnp.dot(
            jnp.concatenate([high, mid, low], axis=0),
            one_hot,
            preferred_element_type=F32,
        )
        columns.append(
            parts[:rows] + parts[rows : 2 * rows] + parts[2 * rows :]
        )
    picked = jnp.concatenate(columns, axis=1)
    mean = jnp.sum(picked, axis=1, keepdims=True) / pix
    centered = picked - mean
    shift = jnp.sum(centered, axis=1, keepdims=True) / pix
    centered = centered - shift
    mean = mean + shift
    squares = jnp.sum(centered * centered, axis=1, keepdims=True)
    as_row = [
        jnp.transpose(jnp.broadcast_to(v, (rows, 128)))[:STAT_ROWS]
        for v in (mean, squares)
    ]
    stat = jnp.concatenate(as_row, axis=1)
    whole_ref[:rows], whole_ref[rows:] = centered, stat
    start = 0
    for ref, count in zip(piece_refs, CHUNKS):
        ref[:count] = centered[start : start + count]
        start += count
    piece_refs[0][CHUNKS[0] :] = stat


def pick(library, annulus):
    rows = library.shape[0]
    pix = annulus.shape[0]
    counts = [rows + STAT_ROWS, CHUNKS[0] + STAT_ROWS, *CHUNKS[1:]]
    return pl.pallas_call(
        pick_kernel,
        out_shape=[jax.ShapeDtypeStruct((10,), jnp.int32)]
        + [jax.ShapeDtypeStruct((count, pix), F32) for count in counts],
        out_specs=[pl.BlockSpec(memory_space=pltpu.SMEM)]
        + [pl.BlockSpec(memory_space=pltpu.VMEM)] * len(counts),
        compiler_params=pltpu.CompilerParams(vmem_limit_bytes=VMEM),
        cost_estimate=FREE,
        name="pick",
    )(annulus, library)


def cut_kernel(whole_ref, *refs):
    out_refs = refs[-len(CHUNKS) :]
    rows = whole_ref.shape[0] - STAT_ROWS
    start = 0
    for ref, count in zip(out_refs, CHUNKS):
        ref[:count] = whole_ref[start : start + count]
        start += count
    out_refs[0][CHUNKS[0] :] = whole_ref[rows:]


def cut(whole, after):
    pix = whole.shape[1]
    counts = [CHUNKS[0] + STAT_ROWS, *CHUNKS[1:]]
    vmem = pl.BlockSpec(memory_space=pltpu.VMEM)
    return pl.pallas_call(
        cut_kernel,
        in_specs=[vmem] + [pl.BlockSpec(memory_space=pl.ANY)] * len(after),
        out_specs=[vmem] * len(counts),
        out_shape=[jax.ShapeDtypeStruct((count, pix), F32) for count in counts],
        compiler_params=pltpu.CompilerParams(vmem_limit_bytes=SMALL),
        cost_estimate=FREE,
        name="cut",
    )(whole, *after)


def choose_kernel(j, first_ref, a_ref, b_ref, *refs):
    keep_ref, send_ref = refs[-2:]
    first = first_ref[j] == 1
    a, b = a_ref[...], b_ref[...]
    keep_ref[...] = jnp.where(first, a, b)
    send_ref[...] = jnp.where(first, b, a)


def choose(j, spots, a, b, after):
    vmem = pl.BlockSpec(memory_space=pltpu.VMEM)
    return pl.pallas_call(
        functools.partial(choose_kernel, j),
        in_specs=[pl.BlockSpec(memory_space=pltpu.SMEM), vmem, vmem]
        + [pl.BlockSpec(memory_space=pl.ANY)] * len(after),
        out_specs=[vmem] * 2,
        out_shape=[jax.ShapeDtypeStruct(a.shape, a.dtype)] * 2,
        compiler_params=pltpu.CompilerParams(vmem_limit_bytes=SMALL),
        cost_estimate=FREE,
        name="choose",
    )(spots, a, b, *after)


def pair_kernel(a_ref, b_ref, *refs):
    refs[-1][0], refs[-1][1] = a_ref[...], b_ref[...]


def pair(a, b, after):
    vmem = pl.BlockSpec(memory_space=pltpu.VMEM)
    return pl.pallas_call(
        pair_kernel,
        in_specs=[vmem] * 2 + [pl.BlockSpec(memory_space=pl.ANY)] * len(after),
        out_specs=vmem,
        out_shape=jax.ShapeDtypeStruct((2,) + a.shape, a.dtype),
        compiler_params=pltpu.CompilerParams(vmem_limit_bytes=SMALL),
        cost_estimate=FREE,
        name="pair",
    )(a, b, *after)


def normalize(a, b, a_stat, b_stat, start):
    count, pix = a.shape
    rows = a_stat.shape[1] // 2
    mean = slice(start, start + count)
    squares = slice(rows + start, rows + start + count)
    gap = (a_stat[:, mean] - b_stat[:, mean]) / 2
    total = a_stat[:, squares] + b_stat[:, squares] + (2 * pix) * (gap * gap)
    scale = 1 / jnp.sqrt(total + EPS)
    gap, scale = [
        jnp.transpose(jnp.broadcast_to(v, (128, count)))[:, :1] for v in (gap, scale)
    ]
    return jnp.concatenate([(a + gap) * scale, (b - gap) * scale], axis=1)


def rows_kernel(a_ref, b_ref, out_ref):
    rows = a_ref.shape[0] - STAT_ROWS
    unit = normalize(
        a_ref[:rows], b_ref[:rows], a_ref[rows : rows + 1], b_ref[rows : rows + 1], 0
    )
    out_ref[:rows], out_ref[rows:] = split(unit)


def unit_rows(a, b):
    rows, pix = a.shape[0] - STAT_ROWS, a.shape[1]
    return pl.pallas_call(
        rows_kernel,
        out_shape=jax.ShapeDtypeStruct((2 * rows, 2 * pix), BF16),
        compiler_params=pltpu.CompilerParams(vmem_limit_bytes=12 << 20),
        cost_estimate=FREE,
        name="unit_rows",
    )(a, b)


def product_kernel(start, count, *refs):
    rows_refs, refs = refs[:2], refs[2:]
    keep, received, pair = refs[:3]
    columns = [keep[...], received[...], pair[0], pair[1]]
    if start == 0:
        stats = [a[count : count + 1] for a in columns]
    else:
        stats = [refs[3][0:1], refs[4][0:1], refs[5][0, 0:1], refs[5][1, 0:1]]
    outs = refs[-2:]
    unit = jnp.concatenate(
        [
            normalize(
                columns[c][:count], columns[c + 1][:count], stats[c], stats[c + 1], start
            )
            for c in (0, 2)
        ],
        axis=0,
    )
    high, low = split(unit)
    dot = functools.partial(
        lax.dot_general,
        dimension_numbers=(((1,), (1,)), ((), ())),
        preferred_element_type=F32,
    )
    for rows_ref, out_ref in zip(rows_refs, outs):
        rows = rows_ref.shape[0] // 2
        both = dot(rows_ref[...], high)
        out_ref[...] = both[:rows] + (both[rows:] + dot(rows_ref[:rows], low))


def product(i, near, far, columns, first, after):
    double, depth = near.shape
    start, count = sum(CHUNKS[:i]), CHUNKS[i]
    vmem = pl.BlockSpec(memory_space=pltpu.VMEM)
    in_specs = [vmem] * 5
    operands = [near, far, *columns]
    if i:
        at, pix = CHUNKS[0] // STAT_ROWS, depth // 2
        in_specs += [pl.BlockSpec((STAT_ROWS, pix), lambda i: (at, 0))] * 2
        in_specs.append(pl.BlockSpec((2, STAT_ROWS, pix), lambda i: (0, at, 0)))
        operands += first
    in_specs += [pl.BlockSpec(memory_space=pl.ANY)] * len(after)
    operands += after
    out = jax.ShapeDtypeStruct((double // 2, 2 * count), F32)
    return pl.pallas_call(
        functools.partial(product_kernel, start, count),
        grid=(1,),
        in_specs=in_specs,
        out_specs=[vmem] * 2,
        out_shape=[out] * 2,
        compiler_params=pltpu.CompilerParams(vmem_limit_bytes=16 << 20),
        cost_estimate=FREE,
        name="product",
    )(*operands)


def place_kernel(at_ref, *refs):
    out_ref = refs[-1]
    n = (len(refs) - 1) // 2
    for side in range(2):

        @pl.when(pl.program_id(0) // 2 == side)
        def _():
            parts = [ref[...] for ref in refs[side * n : side * n + n]]
            out_ref[...] = parts[0] if n == 1 else jnp.concatenate(parts, axis=1)


def place(j, k, spots, own, far, frames, out):
    rows = own[0].shape[0]
    counts = [a.shape[1] // 2 for a in own]
    width = sum(counts)
    in_specs = [pl.BlockSpec((rows, count), lambda i, at: (0, i % 2)) for count in counts]
    in_specs += in_specs
    operands = [spots, *own, *far]
    alias = {}
    if out is not None:
        in_specs.append(pl.BlockSpec(memory_space=pl.ANY))
        alias = {len(operands): 0}
        operands.append(out)
    return pl.pallas_call(
        place_kernel,
        grid_spec=pltpu.PrefetchScalarGridSpec(
            num_scalar_prefetch=1,
            grid=(4,),
            in_specs=in_specs,
            out_specs=pl.BlockSpec(
                (rows, width),
                lambda i, at: (0, at[2 + 4 * j + i] * (rows // width) + (k or 0)),
            ),
        ),
        out_shape=jax.ShapeDtypeStruct((rows, frames * rows), F32),
        input_output_aliases=alias,
        compiler_params=pltpu.CompilerParams(vmem_limit_bytes=10 << 20),
        cost_estimate=FREE,
        name="place",
    )(*operands)


def local_pair(library, annulus):
    frames = lax.axis_size("frame")

    def swap_x(a):
        return lax.ppermute(a, "pix", [(0, 1), (1, 0)])

    def swap_y(a):
        return lax.ppermute(a, "frame", [(f, f ^ 2) for f in range(frames)])

    def swap_core(a):
        return lax.ppermute(a, "frame", [(f, f ^ 1) for f in range(frames)])

    def next_z(a):
        return lax.ppermute(a, "frame", [(f, (f + 4) % frames) for f in range(frames)])

    def previous_z(a):
        return lax.ppermute(a, "frame", [((f + 4) % frames, f) for f in range(frames)])

    spots, whole, *chunks = pick(library, annulus)

    other, far = swap_x(whole), swap_y(whole)
    back_z = [previous_z(a) for a in chunks]
    ring = [chunks, cut(next_z(whole), [other, far, back_z[0]])]
    ring += [[next_z(a) for a in ring[1]], back_z]

    far_other = swap_y(other)
    near = unit_rows(whole, other)
    far = unit_rows(far, far_other)

    keep, chosen, received, paired, columns = {}, {}, {}, {}, {}
    own, sent, back = {}, {}, {}

    def send(j, k, *after):
        keep[j, k], chosen[j, k] = choose(1 - j, spots, ring[1 - j][k], ring[3 - j][k], after)
        received[j, k] = swap_x(chosen[j, k])

    def share(j, k, *after):
        paired[j, k] = pair(keep[j, k], received[j, k], after)
        columns[j, k] = [keep[j, k], received[j, k], swap_core(paired[j, k])]

    def multiply(j, k, *after):
        own[j, k], sent[j, k] = product(k, near, far, columns[j, k], columns[j, 0], after)
        back[j, k] = swap_y(sent[j, k])

    send(0, 0)
    send(0, 1)
    share(0, 0)
    multiply(0, 0)
    share(0, 1)
    send(0, 2)
    multiply(0, 1)
    share(0, 2, sent[0, 0], far_other)
    multiply(0, 2)
    send(1, 0)
    send(1, 1, sent[0, 1], back[0, 0], sent[0, 2])
    send(1, 2, sent[0, 2])
    share(1, 0, back[0, 0])
    multiply(1, 0)
    share(1, 1, back[0, 1])
    multiply(1, 1, sent[0, 0])
    share(1, 2, back[0, 2])
    multiply(1, 2)
    n = len(CHUNKS)
    out = place(
        1, None, spots, [own[0, k] for k in range(n)], [back[0, k] for k in range(n)],
        frames // 2, None,
    )
    for k in range(n):
        out = place(0, k, spots, [own[1, k]], [back[1, k]], frames // 2, out)
    return out


def local(library, annulus):
    picked = jnp.take(library, annulus, axis=1)
    total = lax.psum(jnp.sum(picked, axis=1), "pix")
    frame_mean = total / PIX
    centered = picked - frame_mean[:, None]
    squares = lax.psum(jnp.sum(centered * centered, axis=1), "pix")
    unit = centered / jnp.sqrt(squares + EPS)[:, None]
    partial_gram = lax.dot_general(
        unit,
        lax.all_gather(unit, "frame", axis=0, tiled=True),
        (((1,), (1,)), ((), ())),
        precision=lax.Precision.HIGHEST,
        preferred_element_type=jnp.float32,
    )
    return lax.psum_scatter(partial_gram, "pix", scatter_dimension=1, tiled=True)


def solution(mesh):
    placed = (P("frame", "pix"), P("pix"))
    pair = mesh.shape["pix"] == 2 and mesh.shape["frame"] == 16
    return jax.shard_map(
        local_pair if pair else local,
        mesh=mesh, in_specs=placed, out_specs=P("frame", "pix"), check_vma=False,
    )
```

```python
import functools

import jax
import jax.numpy as jnp
from jax import lax
from jax.experimental import pallas as pl
from jax.experimental.pallas import tpu as pltpu
from jax.sharding import PartitionSpec as P

PIX = 1536
EPS = 1e-06
CHUNKS = (128, 128, 128)
STAT_ROWS = 8
SMALL, VMEM = 6 << 20, 28 << 20
FREE = pl.CostEstimate(flops=1, bytes_accessed=1, transcendentals=0)
F32, BF16 = jnp.float32, jnp.bfloat16


def split(a):
    high = a.astype(BF16)
    return high, (a - high.astype(F32)).astype(BF16)


def pick_kernel(annulus_ref, library_ref, place_ref, whole_ref, *piece_refs):
    rows, band = library_ref.shape
    pix = annulus_ref.shape[0]
    frame, x = lax.axis_index("frame"), lax.axis_index("pix")
    z = frame // 4
    for j in range(2):
        place_ref[j] = jnp.where((z + 4 - j) % 4 // 2 == x, 1, 0)
        for s in range(4):
            place_ref[2 + 4 * j + s] = (z + 4 - j) % 2 * 4 + ((frame % 4) ^ s)
    tile = 256
    width = band - pix + tile
    columns = []
    for start in range(0, pix, tile):
        a = library_ref[:, start : start + width]
        high, rest = split(a)
        mid, low = split(a - high.astype(F32))
        where = annulus_ref[start : start + tile].reshape(1, tile) - start
        one_hot = jnp.where(
            lax.broadcasted_iota(jnp.int32, (width, tile), 0) == where, 1.0, 0.0
        ).astype(BF16)
        parts = jnp.dot(
            jnp.concatenate([high, mid, low], axis=0),
            one_hot,
            preferred_element_type=F32,
        )
        columns.append(
            parts[:rows] + parts[rows : 2 * rows] + parts[2 * rows :]
        )
    picked = jnp.concatenate(columns, axis=1)
    mean = jnp.sum(picked, axis=1, keepdims=True) / pix
    centered = picked - mean
    shift = jnp.sum(centered, axis=1, keepdims=True) / pix
    centered = centered - shift
    mean = mean + shift
    squares = jnp.sum(centered * centered, axis=1, keepdims=True)
    as_row = [
        jnp.transpose(jnp.broadcast_to(v, (rows, 128)))[:STAT_ROWS]
        for v in (mean, squares)
    ]
    stat = jnp.concatenate(as_row, axis=1)
    whole_ref[:rows], whole_ref[rows:] = centered, stat
    start = 0
    for ref, count in zip(piece_refs, CHUNKS):
        ref[:count] = centered[start : start + count]
        start += count
    piece_refs[0][CHUNKS[0] :] = stat


def pick(library, annulus):
    rows = library.shape[0]
    pix = annulus.shape[0]
    counts = [rows + STAT_ROWS, CHUNKS[0] + STAT_ROWS, *CHUNKS[1:]]
    return pl.pallas_call(
        pick_kernel,
        out_shape=[jax.ShapeDtypeStruct((10,), jnp.int32)]
        + [jax.ShapeDtypeStruct((count, pix), F32) for count in counts],
        out_specs=[pl.BlockSpec(memory_space=pltpu.SMEM)]
        + [pl.BlockSpec(memory_space=pltpu.VMEM)] * len(counts),
        compiler_params=pltpu.CompilerParams(vmem_limit_bytes=VMEM),
        cost_estimate=FREE,
        name="pick",
    )(annulus, library)


def cut_kernel(whole_ref, *refs):
    out_refs = refs[-len(CHUNKS) :]
    rows = whole_ref.shape[0] - STAT_ROWS
    start = 0
    for ref, count in zip(out_refs, CHUNKS):
        ref[:count] = whole_ref[start : start + count]
        start += count
    out_refs[0][CHUNKS[0] :] = whole_ref[rows:]


def cut(whole, after):
    pix = whole.shape[1]
    counts = [CHUNKS[0] + STAT_ROWS, *CHUNKS[1:]]
    vmem = pl.BlockSpec(memory_space=pltpu.VMEM)
    return pl.pallas_call(
        cut_kernel,
        in_specs=[vmem] + [pl.BlockSpec(memory_space=pl.ANY)] * len(after),
        out_specs=[vmem] * len(counts),
        out_shape=[jax.ShapeDtypeStruct((count, pix), F32) for count in counts],
        compiler_params=pltpu.CompilerParams(vmem_limit_bytes=SMALL),
        cost_estimate=FREE,
        name="cut",
    )(whole, *after)


def choose_kernel(j, first_ref, a_ref, b_ref, *refs):
    keep_ref, send_ref = refs[-2:]
    first = first_ref[j] == 1
    a, b = a_ref[...], b_ref[...]
    keep_ref[...] = jnp.where(first, a, b)
    send_ref[...] = jnp.where(first, b, a)


def choose(j, spots, a, b, after):
    vmem = pl.BlockSpec(memory_space=pltpu.VMEM)
    return pl.pallas_call(
        functools.partial(choose_kernel, j),
        in_specs=[pl.BlockSpec(memory_space=pltpu.SMEM), vmem, vmem]
        + [pl.BlockSpec(memory_space=pl.ANY)] * len(after),
        out_specs=[vmem] * 2,
        out_shape=[jax.ShapeDtypeStruct(a.shape, a.dtype)] * 2,
        compiler_params=pltpu.CompilerParams(vmem_limit_bytes=SMALL),
        cost_estimate=FREE,
        name="choose",
    )(spots, a, b, *after)


def pair_kernel(a_ref, b_ref, *refs):
    refs[-1][0], refs[-1][1] = a_ref[...], b_ref[...]


def pair(a, b, after):
    vmem = pl.BlockSpec(memory_space=pltpu.VMEM)
    return pl.pallas_call(
        pair_kernel,
        in_specs=[vmem] * 2 + [pl.BlockSpec(memory_space=pl.ANY)] * len(after),
        out_specs=vmem,
        out_shape=jax.ShapeDtypeStruct((2,) + a.shape, a.dtype),
        compiler_params=pltpu.CompilerParams(vmem_limit_bytes=SMALL),
        cost_estimate=FREE,
        name="pair",
    )(a, b, *after)


def normalize(a, b, a_stat, b_stat, start):
    count, pix = a.shape
    rows = a_stat.shape[1] // 2
    mean = slice(start, start + count)
    squares = slice(rows + start, rows + start + count)
    gap = (a_stat[:, mean] - b_stat[:, mean]) / 2
    total = a_stat[:, squares] + b_stat[:, squares] + (2 * pix) * (gap * gap)
    scale = 1 / jnp.sqrt(total + EPS)
    gap, scale = [
        jnp.transpose(jnp.broadcast_to(v, (128, count)))[:, :1] for v in (gap, scale)
    ]
    return jnp.concatenate([(a + gap) * scale, (b - gap) * scale], axis=1)


def rows_kernel(a_ref, b_ref, out_ref):
    rows = a_ref.shape[0] - STAT_ROWS
    unit = normalize(
        a_ref[:rows], b_ref[:rows], a_ref[rows : rows + 1], b_ref[rows : rows + 1], 0
    )
    out_ref[:rows], out_ref[rows:] = split(unit)


def unit_rows(a, b):
    rows, pix = a.shape[0] - STAT_ROWS, a.shape[1]
    return pl.pallas_call(
        rows_kernel,
        out_shape=jax.ShapeDtypeStruct((2 * rows, 2 * pix), BF16),
        compiler_params=pltpu.CompilerParams(vmem_limit_bytes=12 << 20),
        cost_estimate=FREE,
        name="unit_rows",
    )(a, b)


def product_kernel(start, count, *refs):
    rows_refs, refs = refs[:2], refs[2:]
    keep, received, pair = refs[:3]
    columns = [keep[...], received[...], pair[0], pair[1]]
    if start == 0:
        stats = [a[count : count + 1] for a in columns]
    else:
        stats = [refs[3][0:1], refs[4][0:1], refs[5][0, 0:1], refs[5][1, 0:1]]
    outs = refs[-2:]
    unit = jnp.concatenate(
        [
            normalize(
                columns[c][:count], columns[c + 1][:count], stats[c], stats[c + 1], start
            )
            for c in (0, 2)
        ],
        axis=0,
    )
    high, low = split(unit)
    dot = functools.partial(
        lax.dot_general,
        dimension_numbers=(((1,), (1,)), ((), ())),
        preferred_element_type=F32,
    )
    for rows_ref, out_ref in zip(rows_refs, outs):
        rows = rows_ref.shape[0] // 2
        both = dot(rows_ref[...], high)
        out_ref[...] = both[:rows] + (both[rows:] + dot(rows_ref[:rows], low))


def product(i, near, far, columns, first, after):
    double, depth = near.shape
    start, count = sum(CHUNKS[:i]), CHUNKS[i]
    vmem = pl.BlockSpec(memory_space=pltpu.VMEM)
    in_specs = [vmem] * 5
    operands = [near, far, *columns]
    if i:
        at, pix = CHUNKS[0] // STAT_ROWS, depth // 2
        in_specs += [pl.BlockSpec((STAT_ROWS, pix), lambda i: (at, 0))] * 2
        in_specs.append(pl.BlockSpec((2, STAT_ROWS, pix), lambda i: (0, at, 0)))
        operands += first
    in_specs += [pl.BlockSpec(memory_space=pl.ANY)] * len(after)
    operands += after
    out = jax.ShapeDtypeStruct((double // 2, 2 * count), F32)
    return pl.pallas_call(
        functools.partial(product_kernel, start, count),
        grid=(1,),
        in_specs=in_specs,
        out_specs=[vmem] * 2,
        out_shape=[out] * 2,
        compiler_params=pltpu.CompilerParams(vmem_limit_bytes=16 << 20),
        cost_estimate=FREE,
        name="product",
    )(*operands)


def place_kernel(sides, n, at_ref, *refs):
    out_ref = refs[-1]
    for side in range(sides):

        @pl.when(pl.program_id(0) // 2 == side)
        def _():
            parts = [ref[...] for ref in refs[side * n : side * n + n]]
            out_ref[...] = parts[0] if n == 1 else jnp.concatenate(parts, axis=1)


def place(j, k, spots, own, far, frames, out):
    parts = own or far
    sides = bool(own) + bool(far)
    first = 2 + 4 * j + (0 if own else 2)
    rows = parts[0].shape[0]
    counts = [a.shape[1] // 2 for a in parts]
    width = sum(counts)
    in_specs = [pl.BlockSpec((rows, count), lambda i, at: (0, i % 2)) for count in counts]
    in_specs = in_specs * sides
    operands = [spots, *own, *far]
    alias = {}
    if out is not None:
        in_specs.append(pl.BlockSpec(memory_space=pl.ANY))
        alias = {len(operands): 0}
        operands.append(out)
    return pl.pallas_call(
        functools.partial(place_kernel, sides, len(parts)),
        grid_spec=pltpu.PrefetchScalarGridSpec(
            num_scalar_prefetch=1,
            grid=(2 * sides,),
            in_specs=in_specs,
            out_specs=pl.BlockSpec(
                (rows, width),
                lambda i, at: (0, at[first + i] * (rows // width) + (k or 0)),
            ),
        ),
        out_shape=jax.ShapeDtypeStruct((rows, frames * rows), F32),
        input_output_aliases=alias,
        compiler_params=pltpu.CompilerParams(vmem_limit_bytes=10 << 20),
        cost_estimate=FREE,
        name="place",
    )(*operands)


def local_pair(library, annulus):
    frames = lax.axis_size("frame")

    def swap_x(a):
        return lax.ppermute(a, "pix", [(0, 1), (1, 0)])

    def swap_y(a):
        return lax.ppermute(a, "frame", [(f, f ^ 2) for f in range(frames)])

    def swap_core(a):
        return lax.ppermute(a, "frame", [(f, f ^ 1) for f in range(frames)])

    def next_z(a):
        return lax.ppermute(a, "frame", [(f, (f + 4) % frames) for f in range(frames)])

    def previous_z(a):
        return lax.ppermute(a, "frame", [((f + 4) % frames, f) for f in range(frames)])

    spots, whole, *chunks = pick(library, annulus)

    other, far = swap_x(whole), swap_y(whole)
    back_z = [previous_z(a) for a in chunks]
    ring = [chunks, cut(next_z(whole), [other, far, back_z[0]])]
    ring += [[next_z(a) for a in ring[1]], back_z]

    far_other = swap_y(other)
    near = unit_rows(whole, other)
    far = unit_rows(far, far_other)

    keep, chosen, received, paired, columns = {}, {}, {}, {}, {}
    own, sent, back = {}, {}, {}

    def send(j, k, *after):
        keep[j, k], chosen[j, k] = choose(1 - j, spots, ring[1 - j][k], ring[3 - j][k], after)
        received[j, k] = swap_x(chosen[j, k])

    def share(j, k, *after):
        paired[j, k] = pair(keep[j, k], received[j, k], after)
        columns[j, k] = [keep[j, k], received[j, k], swap_core(paired[j, k])]

    def multiply(j, k, *after):
        own[j, k], sent[j, k] = product(k, near, far, columns[j, k], columns[j, 0], after)
        back[j, k] = swap_y(sent[j, k])

    send(0, 0)
    send(0, 1)
    share(0, 0)
    multiply(0, 0)
    share(0, 1)
    send(0, 2)
    multiply(0, 1)
    share(0, 2, sent[0, 0], far_other)
    multiply(0, 2)
    send(1, 0)
    send(1, 1, sent[0, 1], back[0, 0], sent[0, 2])
    send(1, 2, sent[0, 2])
    share(1, 0, back[0, 0])
    multiply(1, 0)
    share(1, 1, back[0, 1])
    multiply(1, 1, sent[0, 0])
    share(1, 2, back[0, 2])
    multiply(1, 2)
    n = len(CHUNKS)
    out = place(
        1, None, spots, [own[0, k] for k in range(n)], [back[0, k] for k in range(n)],
        frames // 2, None,
    )
    for k in range(n):
        out = place(0, k, spots, [own[1, k]], [], frames // 2, out)
    for k in range(n):
        out = place(0, k, spots, [], [back[1, k]], frames // 2, out)
    return out


def local(library, annulus):
    picked = jnp.take(library, annulus, axis=1)
    total = lax.psum(jnp.sum(picked, axis=1), "pix")
    frame_mean = total / PIX
    centered = picked - frame_mean[:, None]
    squares = lax.psum(jnp.sum(centered * centered, axis=1), "pix")
    unit = centered / jnp.sqrt(squares + EPS)[:, None]
    partial_gram = lax.dot_general(
        unit,
        lax.all_gather(unit, "frame", axis=0, tiled=True),
        (((1,), (1,)), ((), ())),
        precision=lax.Precision.HIGHEST,
        preferred_element_type=jnp.float32,
    )
    return lax.psum_scatter(partial_gram, "pix", scatter_dimension=1, tiled=True)


def solution(mesh):
    placed = (P("frame", "pix"), P("pix"))
    pair = mesh.shape["pix"] == 2 and mesh.shape["frame"] == 16
    return jax.shard_map(
        local_pair if pair else local,
        mesh=mesh, in_specs=placed, out_specs=P("frame", "pix"), check_vma=False,
    )
```

```python
import functools

import jax
import jax.numpy as jnp
from jax import lax
from jax.experimental import pallas as pl
from jax.experimental.pallas import tpu as pltpu
from jax.sharding import PartitionSpec as P

PIX = 1536
EPS = 1e-06
CHUNKS = (128, 128, 128)
STAT_ROWS = 8
SMALL, VMEM = 6 << 20, 28 << 20
FREE = pl.CostEstimate(flops=1, bytes_accessed=1, transcendentals=0)
F32, BF16 = jnp.float32, jnp.bfloat16


def split(a):
    high = a.astype(BF16)
    return high, (a - high.astype(F32)).astype(BF16)


def pick_kernel(annulus_ref, library_ref, place_ref, whole_ref, *piece_refs):
    rows, band = library_ref.shape
    pix = annulus_ref.shape[0]
    frame, x = lax.axis_index("frame"), lax.axis_index("pix")
    z = frame // 4
    for j in range(2):
        place_ref[j] = jnp.where((z + 4 - j) % 4 // 2 == x, 1, 0)
        for s in range(4):
            place_ref[2 + 4 * j + s] = (z + 4 - j) % 2 * 4 + ((frame % 4) ^ s)
    tile = 256
    width = band - pix + tile
    columns = []
    for start in range(0, pix, tile):
        a = library_ref[:, start : start + width]
        high, rest = split(a)
        mid, low = split(a - high.astype(F32))
        where = annulus_ref[start : start + tile].reshape(1, tile) - start
        one_hot = jnp.where(
            lax.broadcasted_iota(jnp.int32, (width, tile), 0) == where, 1.0, 0.0
        ).astype(BF16)
        parts = jnp.dot(
            jnp.concatenate([high, mid, low], axis=0),
            one_hot,
            preferred_element_type=F32,
        )
        columns.append(
            parts[:rows] + parts[rows : 2 * rows] + parts[2 * rows :]
        )
    picked = jnp.concatenate(columns, axis=1)
    mean = jnp.sum(picked, axis=1, keepdims=True) / pix
    centered = picked - mean
    shift = jnp.sum(centered, axis=1, keepdims=True) / pix
    centered = centered - shift
    mean = mean + shift
    squares = jnp.sum(centered * centered, axis=1, keepdims=True)
    as_row = [
        jnp.transpose(jnp.broadcast_to(v, (rows, 128)))[:STAT_ROWS]
        for v in (mean, squares)
    ]
    stat = jnp.concatenate(as_row, axis=1)
    whole_ref[:rows], whole_ref[rows:] = centered, stat
    start = 0
    for ref, count in zip(piece_refs, CHUNKS):
        ref[:count] = centered[start : start + count]
        start += count
    piece_refs[0][CHUNKS[0] :] = stat


def pick(library, annulus):
    rows = library.shape[0]
    pix = annulus.shape[0]
    counts = [rows + STAT_ROWS, CHUNKS[0] + STAT_ROWS, *CHUNKS[1:]]
    return pl.pallas_call(
        pick_kernel,
        out_shape=[jax.ShapeDtypeStruct((10,), jnp.int32)]
        + [jax.ShapeDtypeStruct((count, pix), F32) for count in counts],
        out_specs=[pl.BlockSpec(memory_space=pltpu.SMEM)]
        + [pl.BlockSpec(memory_space=pltpu.VMEM)] * len(counts),
        compiler_params=pltpu.CompilerParams(vmem_limit_bytes=VMEM),
        cost_estimate=FREE,
        name="pick",
    )(annulus, library)


def cut_kernel(whole_ref, *refs):
    out_refs = refs[-len(CHUNKS) :]
    rows = whole_ref.shape[0] - STAT_ROWS
    start = 0
    for ref, count in zip(out_refs, CHUNKS):
        ref[:count] = whole_ref[start : start + count]
        start += count
    out_refs[0][CHUNKS[0] :] = whole_ref[rows:]


def cut(whole, after):
    pix = whole.shape[1]
    counts = [CHUNKS[0] + STAT_ROWS, *CHUNKS[1:]]
    vmem = pl.BlockSpec(memory_space=pltpu.VMEM)
    return pl.pallas_call(
        cut_kernel,
        in_specs=[vmem] + [pl.BlockSpec(memory_space=pl.ANY)] * len(after),
        out_specs=[vmem] * len(counts),
        out_shape=[jax.ShapeDtypeStruct((count, pix), F32) for count in counts],
        compiler_params=pltpu.CompilerParams(vmem_limit_bytes=SMALL),
        cost_estimate=FREE,
        name="cut",
    )(whole, *after)


def choose_kernel(j, first_ref, a_ref, b_ref, *refs):
    keep_ref, send_ref = refs[-2:]
    first = first_ref[j] == 1
    a, b = a_ref[...], b_ref[...]
    keep_ref[...] = jnp.where(first, a, b)
    send_ref[...] = jnp.where(first, b, a)


def choose(j, spots, a, b, after):
    vmem = pl.BlockSpec(memory_space=pltpu.VMEM)
    return pl.pallas_call(
        functools.partial(choose_kernel, j),
        in_specs=[pl.BlockSpec(memory_space=pltpu.SMEM), vmem, vmem]
        + [pl.BlockSpec(memory_space=pl.ANY)] * len(after),
        out_specs=[vmem] * 2,
        out_shape=[jax.ShapeDtypeStruct(a.shape, a.dtype)] * 2,
        compiler_params=pltpu.CompilerParams(vmem_limit_bytes=SMALL),
        cost_estimate=FREE,
        name="choose",
    )(spots, a, b, *after)


def pair_kernel(a_ref, b_ref, *refs):
    refs[-1][0], refs[-1][1] = a_ref[...], b_ref[...]


def pair(a, b, after):
    vmem = pl.BlockSpec(memory_space=pltpu.VMEM)
    return pl.pallas_call(
        pair_kernel,
        in_specs=[vmem] * 2 + [pl.BlockSpec(memory_space=pl.ANY)] * len(after),
        out_specs=vmem,
        out_shape=jax.ShapeDtypeStruct((2,) + a.shape, a.dtype),
        compiler_params=pltpu.CompilerParams(vmem_limit_bytes=SMALL),
        cost_estimate=FREE,
        name="pair",
    )(a, b, *after)


def normalize(a, b, a_stat, b_stat, start):
    count, pix = a.shape
    rows = a_stat.shape[1] // 2
    mean = slice(start, start + count)
    squares = slice(rows + start, rows + start + count)
    gap = (a_stat[:, mean] - b_stat[:, mean]) / 2
    total = a_stat[:, squares] + b_stat[:, squares] + (2 * pix) * (gap * gap)
    scale = 1 / jnp.sqrt(total + EPS)
    gap, scale = [
        jnp.transpose(jnp.broadcast_to(v, (128, count)))[:, :1] for v in (gap, scale)
    ]
    return jnp.concatenate([(a + gap) * scale, (b - gap) * scale], axis=1)


def rows_kernel(a_ref, b_ref, out_ref):
    rows = a_ref.shape[0] - STAT_ROWS
    unit = normalize(
        a_ref[:rows], b_ref[:rows], a_ref[rows : rows + 1], b_ref[rows : rows + 1], 0
    )
    out_ref[:rows], out_ref[rows:] = split(unit)


def unit_rows(a, b):
    rows, pix = a.shape[0] - STAT_ROWS, a.shape[1]
    return pl.pallas_call(
        rows_kernel,
        out_shape=jax.ShapeDtypeStruct((2 * rows, 2 * pix), BF16),
        compiler_params=pltpu.CompilerParams(vmem_limit_bytes=12 << 20),
        cost_estimate=FREE,
        name="unit_rows",
    )(a, b)


def product_kernel(start, count, *refs):
    rows_refs, refs = refs[:2], refs[2:]
    keep, received, pair = refs[:3]
    columns = [keep[...], received[...], pair[0], pair[1]]
    if start == 0:
        stats = [a[count : count + 1] for a in columns]
    else:
        stats = [refs[3][0:1], refs[4][0:1], refs[5][0, 0:1], refs[5][1, 0:1]]
    outs = refs[-2:]
    unit = jnp.concatenate(
        [
            normalize(
                columns[c][:count], columns[c + 1][:count], stats[c], stats[c + 1], start
            )
            for c in (0, 2)
        ],
        axis=0,
    )
    high, low = split(unit)
    dot = functools.partial(
        lax.dot_general,
        dimension_numbers=(((1,), (1,)), ((), ())),
        preferred_element_type=F32,
    )
    for rows_ref, out_ref in zip(rows_refs, outs):
        rows = rows_ref.shape[0] // 2
        both = dot(rows_ref[...], high)
        out_ref[...] = both[:rows] + (both[rows:] + dot(rows_ref[:rows], low))


def product(i, near, far, columns, first, after):
    double, depth = near.shape
    start, count = sum(CHUNKS[:i]), CHUNKS[i]
    vmem = pl.BlockSpec(memory_space=pltpu.VMEM)
    in_specs = [vmem] * 5
    operands = [near, far, *columns]
    if i:
        at, pix = CHUNKS[0] // STAT_ROWS, depth // 2
        in_specs += [pl.BlockSpec((STAT_ROWS, pix), lambda i: (at, 0))] * 2
        in_specs.append(pl.BlockSpec((2, STAT_ROWS, pix), lambda i: (0, at, 0)))
        operands += first
    in_specs += [pl.BlockSpec(memory_space=pl.ANY)] * len(after)
    operands += after
    out = jax.ShapeDtypeStruct((double // 2, 2 * count), F32)
    return pl.pallas_call(
        functools.partial(product_kernel, start, count),
        grid=(1,),
        in_specs=in_specs,
        out_specs=[vmem] * 2,
        out_shape=[out] * 2,
        compiler_params=pltpu.CompilerParams(vmem_limit_bytes=16 << 20),
        cost_estimate=FREE,
        name="product",
    )(*operands)


def place_kernel(sides, n, at_ref, *refs):
    out_ref = refs[-1]
    for side in range(sides):

        @pl.when(pl.program_id(0) // 2 == side)
        def _():
            parts = [ref[...] for ref in refs[side * n : side * n + n]]
            out_ref[...] = parts[0] if n == 1 else jnp.concatenate(parts, axis=1)


def place(j, k, spots, own, far, frames, out):
    parts = own or far
    sides = bool(own) + bool(far)
    first = 2 + 4 * j + (0 if own else 2)
    rows = parts[0].shape[0]
    counts = [a.shape[1] // 2 for a in parts]
    width = sum(counts)
    in_specs = [pl.BlockSpec((rows, count), lambda i, at: (0, i % 2)) for count in counts]
    in_specs = in_specs * sides
    operands = [spots, *own, *far]
    alias = {}
    if out is not None:
        in_specs.append(pl.BlockSpec(memory_space=pl.ANY))
        alias = {len(operands): 0}
        operands.append(out)
    return pl.pallas_call(
        functools.partial(place_kernel, sides, len(parts)),
        grid_spec=pltpu.PrefetchScalarGridSpec(
            num_scalar_prefetch=1,
            grid=(2 * sides,),
            in_specs=in_specs,
            out_specs=pl.BlockSpec(
                (rows, width),
                lambda i, at: (0, at[first + i] * (rows // width) + (k or 0)),
            ),
        ),
        out_shape=jax.ShapeDtypeStruct((rows, frames * rows), F32),
        input_output_aliases=alias,
        compiler_params=pltpu.CompilerParams(vmem_limit_bytes=10 << 20),
        cost_estimate=FREE,
        name="place",
    )(*operands)


def local_pair(library, annulus):
    frames = lax.axis_size("frame")

    def swap_x(a):
        return lax.ppermute(a, "pix", [(0, 1), (1, 0)])

    def swap_y(a):
        return lax.ppermute(a, "frame", [(f, f ^ 2) for f in range(frames)])

    def swap_core(a):
        return lax.ppermute(a, "frame", [(f, f ^ 1) for f in range(frames)])

    def next_z(a):
        return lax.ppermute(a, "frame", [(f, (f + 4) % frames) for f in range(frames)])

    def previous_z(a):
        return lax.ppermute(a, "frame", [((f + 4) % frames, f) for f in range(frames)])

    spots, whole, *chunks = pick(library, annulus)

    other, far = swap_x(whole), swap_y(whole)
    back_z = [previous_z(a) for a in chunks]
    ring = [chunks, cut(next_z(whole), [other, far, back_z[0]])]
    ring += [[next_z(a) for a in ring[1]], back_z]

    far_other = swap_y(other)
    near = unit_rows(whole, other)
    far = unit_rows(far, far_other)

    keep, chosen, received, paired, columns = {}, {}, {}, {}, {}
    own, sent, back = {}, {}, {}

    def send(j, k, *after):
        keep[j, k], chosen[j, k] = choose(1 - j, spots, ring[1 - j][k], ring[3 - j][k], after)
        received[j, k] = swap_x(chosen[j, k])

    def share(j, k, *after):
        paired[j, k] = pair(keep[j, k], received[j, k], after)
        columns[j, k] = [keep[j, k], received[j, k], swap_core(paired[j, k])]

    def multiply(j, k, *after):
        own[j, k], sent[j, k] = product(k, near, far, columns[j, k], columns[j, 0], after)
        back[j, k] = swap_y(sent[j, k])

    send(0, 0)
    send(0, 1)
    share(0, 0)
    multiply(0, 0)
    share(0, 1, far_other)
    send(0, 2)
    multiply(0, 1)
    share(0, 2, sent[0, 0], far_other)
    multiply(0, 2)
    send(1, 0)
    send(1, 1, sent[0, 1], back[0, 0], sent[0, 2])
    send(1, 2, sent[0, 2])
    share(1, 0, back[0, 0])
    multiply(1, 0)
    share(1, 1, back[0, 1])
    multiply(1, 1, sent[0, 0])
    share(1, 2, back[0, 2])
    multiply(1, 2)
    n = len(CHUNKS)
    out = place(
        1, None, spots, [own[0, k] for k in range(n)], [back[0, k] for k in range(n)],
        frames // 2, None,
    )
    for k in range(n):
        out = place(0, k, spots, [own[1, k]], [], frames // 2, out)
    for k in range(n):
        out = place(0, k, spots, [], [back[1, k]], frames // 2, out)
    return out


def local(library, annulus):
    picked = jnp.take(library, annulus, axis=1)
    total = lax.psum(jnp.sum(picked, axis=1), "pix")
    frame_mean = total / PIX
    centered = picked - frame_mean[:, None]
    squares = lax.psum(jnp.sum(centered * centered, axis=1), "pix")
    unit = centered / jnp.sqrt(squares + EPS)[:, None]
    partial_gram = lax.dot_general(
        unit,
        lax.all_gather(unit, "frame", axis=0, tiled=True),
        (((1,), (1,)), ((), ())),
        precision=lax.Precision.HIGHEST,
        preferred_element_type=jnp.float32,
    )
    return lax.psum_scatter(partial_gram, "pix", scatter_dimension=1, tiled=True)


def solution(mesh):
    placed = (P("frame", "pix"), P("pix"))
    pair = mesh.shape["pix"] == 2 and mesh.shape["frame"] == 16
    return jax.shard_map(
        local_pair if pair else local,
        mesh=mesh, in_specs=placed, out_specs=P("frame", "pix"), check_vma=False,
    )
```

```python
import functools

import jax
import jax.numpy as jnp
from jax import lax
from jax.experimental import pallas as pl
from jax.experimental.pallas import tpu as pltpu
from jax.sharding import PartitionSpec as P

PIX = 1536
EPS = 1e-06
CHUNKS = (128, 128, 128)
STAT_ROWS = 8
SMALL, VMEM = 6 << 20, 28 << 20
FREE = pl.CostEstimate(flops=1, bytes_accessed=1, transcendentals=0)
F32, BF16 = jnp.float32, jnp.bfloat16


def split(a):
    high = a.astype(BF16)
    return high, (a - high.astype(F32)).astype(BF16)


def pick_kernel(annulus_ref, library_ref, place_ref, whole_ref, *piece_refs):
    rows, band = library_ref.shape
    pix = annulus_ref.shape[0]
    frame, x = lax.axis_index("frame"), lax.axis_index("pix")
    z = frame // 4
    for j in range(2):
        place_ref[j] = jnp.where((z + 4 - j) % 4 // 2 == x, 1, 0)
        for s in range(4):
            place_ref[2 + 4 * j + s] = (z + 4 - j) % 2 * 4 + ((frame % 4) ^ s)
    tile = 256
    width = band - pix + tile
    columns = []
    for start in range(0, pix, tile):
        a = library_ref[:, start : start + width]
        high, rest = split(a)
        mid, low = split(a - high.astype(F32))
        where = annulus_ref[start : start + tile].reshape(1, tile) - start
        one_hot = jnp.where(
            lax.broadcasted_iota(jnp.int32, (width, tile), 0) == where, 1.0, 0.0
        ).astype(BF16)
        parts = jnp.dot(
            jnp.concatenate([high, mid, low], axis=0),
            one_hot,
            preferred_element_type=F32,
        )
        columns.append(
            parts[:rows] + parts[rows : 2 * rows] + parts[2 * rows :]
        )
    picked = jnp.concatenate(columns, axis=1)
    mean = jnp.sum(picked, axis=1, keepdims=True) / pix
    centered = picked - mean
    shift = jnp.sum(centered, axis=1, keepdims=True) / pix
    centered = centered - shift
    mean = mean + shift
    squares = jnp.sum(centered * centered, axis=1, keepdims=True)
    as_row = [
        jnp.transpose(jnp.broadcast_to(v, (rows, 128)))[:STAT_ROWS]
        for v in (mean, squares)
    ]
    stat = jnp.concatenate(as_row, axis=1)
    whole_ref[:rows], whole_ref[rows:] = centered, stat
    start = 0
    for ref, count in zip(piece_refs, CHUNKS):
        ref[:count] = centered[start : start + count]
        start += count
    piece_refs[0][CHUNKS[0] :] = stat


def pick(library, annulus):
    rows = library.shape[0]
    pix = annulus.shape[0]
    counts = [rows + STAT_ROWS, CHUNKS[0] + STAT_ROWS, *CHUNKS[1:]]
    return pl.pallas_call(
        pick_kernel,
        out_shape=[jax.ShapeDtypeStruct((10,), jnp.int32)]
        + [jax.ShapeDtypeStruct((count, pix), F32) for count in counts],
        out_specs=[pl.BlockSpec(memory_space=pltpu.SMEM)]
        + [pl.BlockSpec(memory_space=pltpu.VMEM)] * len(counts),
        compiler_params=pltpu.CompilerParams(vmem_limit_bytes=VMEM),
        cost_estimate=FREE,
        name="pick",
    )(annulus, library)


def cut_kernel(whole_ref, *refs):
    out_refs = refs[-len(CHUNKS) :]
    rows = whole_ref.shape[0] - STAT_ROWS
    start = 0
    for ref, count in zip(out_refs, CHUNKS):
        ref[:count] = whole_ref[start : start + count]
        start += count
    out_refs[0][CHUNKS[0] :] = whole_ref[rows:]


def cut(whole, after):
    pix = whole.shape[1]
    counts = [CHUNKS[0] + STAT_ROWS, *CHUNKS[1:]]
    vmem = pl.BlockSpec(memory_space=pltpu.VMEM)
    return pl.pallas_call(
        cut_kernel,
        in_specs=[vmem] + [pl.BlockSpec(memory_space=pl.ANY)] * len(after),
        out_specs=[vmem] * len(counts),
        out_shape=[jax.ShapeDtypeStruct((count, pix), F32) for count in counts],
        compiler_params=pltpu.CompilerParams(vmem_limit_bytes=SMALL),
        cost_estimate=FREE,
        name="cut",
    )(whole, *after)


def choose_kernel(j, first_ref, a_ref, b_ref, *refs):
    keep_ref, send_ref = refs[-2:]
    first = first_ref[j] == 1
    a, b = a_ref[...], b_ref[...]
    keep_ref[...] = jnp.where(first, a, b)
    send_ref[...] = jnp.where(first, b, a)


def choose(j, spots, a, b, after):
    vmem = pl.BlockSpec(memory_space=pltpu.VMEM)
    return pl.pallas_call(
        functools.partial(choose_kernel, j),
        in_specs=[pl.BlockSpec(memory_space=pltpu.SMEM), vmem, vmem]
        + [pl.BlockSpec(memory_space=pl.ANY)] * len(after),
        out_specs=[vmem] * 2,
        out_shape=[jax.ShapeDtypeStruct(a.shape, a.dtype)] * 2,
        compiler_params=pltpu.CompilerParams(vmem_limit_bytes=SMALL),
        cost_estimate=FREE,
        name="choose",
    )(spots, a, b, *after)


def pair_kernel(a_ref, b_ref, *refs):
    refs[-1][0], refs[-1][1] = a_ref[...], b_ref[...]


def pair(a, b, after):
    vmem = pl.BlockSpec(memory_space=pltpu.VMEM)
    return pl.pallas_call(
        pair_kernel,
        in_specs=[vmem] * 2 + [pl.BlockSpec(memory_space=pl.ANY)] * len(after),
        out_specs=vmem,
        out_shape=jax.ShapeDtypeStruct((2,) + a.shape, a.dtype),
        compiler_params=pltpu.CompilerParams(vmem_limit_bytes=SMALL),
        cost_estimate=FREE,
        name="pair",
    )(a, b, *after)


def normalize(a, b, a_stat, b_stat, start):
    count, pix = a.shape
    rows = a_stat.shape[1] // 2
    mean = slice(start, start + count)
    squares = slice(rows + start, rows + start + count)
    gap = (a_stat[:, mean] - b_stat[:, mean]) / 2
    total = a_stat[:, squares] + b_stat[:, squares] + (2 * pix) * (gap * gap)
    scale = 1 / jnp.sqrt(total + EPS)
    gap, scale = [
        jnp.transpose(jnp.broadcast_to(v, (128, count)))[:, :1] for v in (gap, scale)
    ]
    return jnp.concatenate([(a + gap) * scale, (b - gap) * scale], axis=1)


def rows_kernel(a_ref, b_ref, out_ref):
    rows = a_ref.shape[0] - STAT_ROWS
    unit = normalize(
        a_ref[:rows], b_ref[:rows], a_ref[rows : rows + 1], b_ref[rows : rows + 1], 0
    )
    out_ref[:rows], out_ref[rows:] = split(unit)


def unit_rows(a, b):
    rows, pix = a.shape[0] - STAT_ROWS, a.shape[1]
    return pl.pallas_call(
        rows_kernel,
        out_shape=jax.ShapeDtypeStruct((2 * rows, 2 * pix), BF16),
        compiler_params=pltpu.CompilerParams(vmem_limit_bytes=12 << 20),
        cost_estimate=FREE,
        name="unit_rows",
    )(a, b)


def product_kernel(start, count, *refs):
    rows_refs, refs = refs[:2], refs[2:]
    keep, received, pair = refs[:3]
    columns = [keep[...], received[...], pair[0], pair[1]]
    if start == 0:
        stats = [a[count : count + 1] for a in columns]
    else:
        stats = [refs[3][0:1], refs[4][0:1], refs[5][0, 0:1], refs[5][1, 0:1]]
    outs = refs[-2:]
    unit = jnp.concatenate(
        [
            normalize(
                columns[c][:count], columns[c + 1][:count], stats[c], stats[c + 1], start
            )
            for c in (0, 2)
        ],
        axis=0,
    )
    high, low = split(unit)
    dot = functools.partial(
        lax.dot_general,
        dimension_numbers=(((1,), (1,)), ((), ())),
        preferred_element_type=F32,
    )
    for rows_ref, out_ref in zip(rows_refs, outs):
        rows = rows_ref.shape[0] // 2
        both = dot(rows_ref[...], high)
        out_ref[...] = both[:rows] + (both[rows:] + dot(rows_ref[:rows], low))


def product(i, near, far, columns, first, after):
    double, depth = near.shape
    start, count = sum(CHUNKS[:i]), CHUNKS[i]
    vmem = pl.BlockSpec(memory_space=pltpu.VMEM)
    in_specs = [vmem] * 5
    operands = [near, far, *columns]
    if i:
        at, pix = CHUNKS[0] // STAT_ROWS, depth // 2
        in_specs += [pl.BlockSpec((STAT_ROWS, pix), lambda i: (at, 0))] * 2
        in_specs.append(pl.BlockSpec((2, STAT_ROWS, pix), lambda i: (0, at, 0)))
        operands += first
    in_specs += [pl.BlockSpec(memory_space=pl.ANY)] * len(after)
    operands += after
    out = jax.ShapeDtypeStruct((double // 2, 2 * count), F32)
    return pl.pallas_call(
        functools.partial(product_kernel, start, count),
        grid=(1,),
        in_specs=in_specs,
        out_specs=[vmem] * 2,
        out_shape=[out] * 2,
        compiler_params=pltpu.CompilerParams(vmem_limit_bytes=16 << 20),
        cost_estimate=FREE,
        name="product",
    )(*operands)


def place_kernel(sides, n, at_ref, *refs):
    out_ref = refs[-1]
    for side in range(sides):

        @pl.when(pl.program_id(0) // 2 == side)
        def _():
            parts = [ref[...] for ref in refs[side * n : side * n + n]]
            out_ref[...] = parts[0] if n == 1 else jnp.concatenate(parts, axis=1)


def place(j, k, spots, own, far, frames, out):
    parts = own or far
    sides = bool(own) + bool(far)
    first = 2 + 4 * j + (0 if own else 2)
    rows = parts[0].shape[0]
    counts = [a.shape[1] // 2 for a in parts]
    width = sum(counts)
    in_specs = [pl.BlockSpec((rows, count), lambda i, at: (0, i % 2)) for count in counts]
    in_specs = in_specs * sides
    operands = [spots, *own, *far]
    alias = {}
    if out is not None:
        in_specs.append(pl.BlockSpec(memory_space=pl.ANY))
        alias = {len(operands): 0}
        operands.append(out)
    return pl.pallas_call(
        functools.partial(place_kernel, sides, len(parts)),
        grid_spec=pltpu.PrefetchScalarGridSpec(
            num_scalar_prefetch=1,
            grid=(2 * sides,),
            in_specs=in_specs,
            out_specs=pl.BlockSpec(
                (rows, width),
                lambda i, at: (0, at[first + i] * (rows // width) + (k or 0)),
            ),
        ),
        out_shape=jax.ShapeDtypeStruct((rows, frames * rows), F32),
        input_output_aliases=alias,
        compiler_params=pltpu.CompilerParams(vmem_limit_bytes=10 << 20),
        cost_estimate=FREE,
        name="place",
    )(*operands)


def local_pair(library, annulus):
    frames = lax.axis_size("frame")

    def swap_x(a):
        return lax.ppermute(a, "pix", [(0, 1), (1, 0)])

    def swap_y(a):
        return lax.ppermute(a, "frame", [(f, f ^ 2) for f in range(frames)])

    def swap_core(a):
        return lax.ppermute(a, "frame", [(f, f ^ 1) for f in range(frames)])

    def next_z(a):
        return lax.ppermute(a, "frame", [(f, (f + 4) % frames) for f in range(frames)])

    def previous_z(a):
        return lax.ppermute(a, "frame", [((f + 4) % frames, f) for f in range(frames)])

    spots, whole, *chunks = pick(library, annulus)

    other, far = swap_x(whole), swap_y(whole)
    back_z = [previous_z(a) for a in chunks]
    ring = [chunks, cut(next_z(whole), [other, far, back_z[0]])]
    ring += [[next_z(a) for a in ring[1]], back_z]

    far_other = swap_y(other)
    near = unit_rows(whole, other)
    far = unit_rows(far, far_other)

    keep, chosen, received, paired, columns = {}, {}, {}, {}, {}
    own, sent, back = {}, {}, {}

    def send(j, k, *after):
        keep[j, k], chosen[j, k] = choose(1 - j, spots, ring[1 - j][k], ring[3 - j][k], after)
        received[j, k] = swap_x(chosen[j, k])

    def share(j, k, *after):
        paired[j, k] = pair(keep[j, k], received[j, k], after)
        columns[j, k] = [keep[j, k], received[j, k], swap_core(paired[j, k])]

    def multiply(j, k, *after):
        own[j, k], sent[j, k] = product(k, near, far, columns[j, k], columns[j, 0], after)
        back[j, k] = swap_y(sent[j, k])

    send(0, 0)
    send(0, 1)
    share(0, 0)
    multiply(0, 0)
    share(0, 1)
    send(0, 2)
    multiply(0, 1)
    share(0, 2, sent[0, 0], far_other)
    multiply(0, 2)
    send(1, 0)
    send(1, 1, sent[0, 1], back[0, 0], sent[0, 2])
    send(1, 2, sent[0, 2])
    share(1, 0, sent[0, 2])
    multiply(1, 0)
    share(1, 1, back[0, 1])
    multiply(1, 1, sent[0, 0])
    share(1, 2, back[0, 2])
    multiply(1, 2)
    n = len(CHUNKS)
    out = place(
        1, None, spots, [own[0, k] for k in range(n)], [back[0, k] for k in range(n)],
        frames // 2, None,
    )
    for k in range(n):
        out = place(0, k, spots, [own[1, k]], [], frames // 2, out)
    for k in range(n):
        out = place(0, k, spots, [], [back[1, k]], frames // 2, out)
    return out


def local(library, annulus):
    picked = jnp.take(library, annulus, axis=1)
    total = lax.psum(jnp.sum(picked, axis=1), "pix")
    frame_mean = total / PIX
    centered = picked - frame_mean[:, None]
    squares = lax.psum(jnp.sum(centered * centered, axis=1), "pix")
    unit = centered / jnp.sqrt(squares + EPS)[:, None]
    partial_gram = lax.dot_general(
        unit,
        lax.all_gather(unit, "frame", axis=0, tiled=True),
        (((1,), (1,)), ((), ())),
        precision=lax.Precision.HIGHEST,
        preferred_element_type=jnp.float32,
    )
    return lax.psum_scatter(partial_gram, "pix", scatter_dimension=1, tiled=True)


def solution(mesh):
    placed = (P("frame", "pix"), P("pix"))
    pair = mesh.shape["pix"] == 2 and mesh.shape["frame"] == 16
    return jax.shard_map(
        local_pair if pair else local,
        mesh=mesh, in_specs=placed, out_specs=P("frame", "pix"), check_vma=False,
    )
```
